32 devices in a mesh: dp: 8 (over z, core), mp: 4 (over y, x).
Axes of the slice: x: 2, y: 2, z: 4, core: 2. Of those that a mesh axis runs over, the one named last changes fastest.
Arguments:
- grad: bfloat16 [8, 4096, 7168], P('dp', 'mp')
- error: bfloat16 [8, 4096, 7168], P('dp', 'mp'), may hold values from -3 to 3
- init_factor: bfloat16 [7168, 128], replicated, may hold values from -0.0625 to 0.0625
Outputs:
- new_error: bfloat16 [8, 4096, 7168], P('dp', 'mp')
- right_factor: bfloat16 [7168, 128], P('mp')
The draws below stay inside these ranges and needn't reach their ends.
All inputs are finite; a program needn't handle non-finite values.
Results may differ from the reference program's by a relative error of at most 0.009.
Values may be sent and summed in bfloat16 or wider, within the bound.
No kernel may reach another device: no remote copies, remote signals or barrier semaphores. Data moves between devices by JAX's collectives and lax.ppermute only.
A program may use at most 128 MiB of HBM per device.

```python
import math
import jax
import jax.numpy as jnp
from jax import lax

D = 4096
FF = 7168
RANK = 128
REPLICAS = 8


def draw_grad(key, part):
    key = jax.random.fold_in(key, 11)
    key_rows, key_cols, key_noise = jax.random.split(key, 3)
    position = jnp.arange(D, dtype=jnp.float32) / D
    rising = jnp.exp(math.log(3.0) * (position - 0.5))
    row_scale = rising * jnp.exp(jax.random.uniform(key_rows, (D,), jnp.float32, -math.log(3.0), math.log(3.0)))
    col_scale = jnp.exp(jax.random.uniform(key_cols, (FF,), jnp.float32, -math.log(3.0), math.log(3.0)))
    values = jax.random.normal(key_noise, (REPLICAS, D, FF), jnp.float32)
    values = values * row_scale[None, :, None] * col_scale[None, None, :]
    return values.astype(jnp.bfloat16)


def shard_levels(stream_key, extent, cuts, low, high):
    def one(axis_at, shards_of):
        steps = jax.random.uniform(jax.random.fold_in(jax.random.fold_in(stream_key, 6), axis_at), (shards_of,), jnp.float32, low / len(cuts), high / len(cuts))
        return jnp.repeat(jnp.exp(steps), extent[axis_at] // shards_of).reshape((-1,) + (1,) * (len(extent) - axis_at - 1))

    factor_of = one(*cuts[0])
    for cut in cuts[1:]:
        factor_of = factor_of * one(*cut)
    return factor_of


def normal_values(key, shape, scale, limit, pieces=(), held_as=jnp.bfloat16):
    gain = shard_levels(key, shape, pieces, -0.22, 0.18) if pieces else 1.0
    entries = jax.random.normal(key, shape, jnp.float32) * scale * gain
    return jnp.minimum(jnp.maximum(entries, -limit), limit).astype(held_as)


def setup_inputs(seed: int = 0) -> dict:
    key_list = jax.random.split(jax.random.key(seed), 4)
    return {
        "grad": draw_grad(jax.random.fold_in(key_list[3], 71), 0),
        "error": normal_values(key_list[1], (REPLICAS, D, FF), 0.5, 3.0, ((0, 8), (1, 4))),
        "init_factor": normal_values(key_list[2], (FF, RANK), FF ** -0.5, 0.0625),
    }


def reference(grad, error, init_factor):
    compensated = (grad.astype(jnp.float32) + error.astype(jnp.float32)).astype(jnp.bfloat16)

    def add_rows(running, replica_block):
        return (running + jnp.dot(replica_block.astype(jnp.float32), init_factor.astype(jnp.float32), preferred_element_type=jnp.float32), None)
    partial_value, _ = lax.scan(add_rows, jnp.zeros((D, RANK), jnp.float32), compensated)
    gram_matrix = jnp.dot(partial_value.T.astype(jnp.float32), partial_value.astype(jnp.float32), precision=lax.Precision.HIGHEST, preferred_element_type=jnp.float32)
    cholesky_factor = jnp.linalg.cholesky(gram_matrix)
    ortho_basis = jax.scipy.linalg.solve_triangular(cholesky_factor, partial_value.T, lower=True).T.astype(jnp.bfloat16)

    def add_cols(running, replica_block):
        product = lax.dot_general(replica_block.astype(jnp.float32), ortho_basis.astype(jnp.float32), (((0,), (0,)), ((), ())), preferred_element_type=jnp.float32)
        return (running + product, None)
    summed, _ = lax.scan(add_cols, jnp.zeros((FF, RANK), jnp.float32), compensated)
    right_side = (summed / REPLICAS).astype(jnp.bfloat16)
    decompressed = lax.dot_general(ortho_basis.astype(jnp.float32), right_side.astype(jnp.float32), (((1,), (1,)), ((), ())), preferred_element_type=jnp.float32)

    def update_one(replica_block):
        return (replica_block.astype(jnp.float32) - decompressed).astype(jnp.bfloat16)
    new_error = lax.map(update_one, compensated)
    return (new_error, right_side)
```

```python
import functools

import jax
import jax.numpy as jnp
from jax import lax
from jax.experimental import pallas as pl
from jax.experimental.pallas import tpu as pltpu
from jax.sharding import PartitionSpec as P

F32 = jnp.float32
BF16 = jnp.bfloat16
LANES = 128
MIB = 1024 * 1024
AXES = ("dp", "mp")


def as_bf16(x):
    rounded = lax.reduce_precision(x, 8, 7)
    return rounded.astype(BF16), rounded


def left_kernel(half_ref, grad_ref, error_ref, init_ref, comp_ref, left_ref):
    del half_ref
    tile = grad_ref.shape[0]
    total = (grad_ref[...].astype(F32) + error_ref[...].astype(F32)).astype(BF16)
    comp_ref[pl.ds(pl.multiple_of(pl.program_id(0) * tile, tile), tile), :] = total
    left_ref[...] = jnp.dot(total, init_ref[...], preferred_element_type=F32)


def left_product(half, grad, error, init):
    rows, cols = grad.shape
    rank = init.shape[1]
    count = rows // 2
    tile = min(128, count)
    steps = count // tile
    return pl.pallas_call(
        left_kernel,
        grid_spec=pltpu.PrefetchScalarGridSpec(
            num_scalar_prefetch=1,
            grid=(steps,),
            in_specs=[
                pl.BlockSpec((tile, cols), lambda i, half: (half[0] * steps + i, 0)),
                pl.BlockSpec((tile, cols), lambda i, half: (half[0] * steps + i, 0)),
                pl.BlockSpec((cols, rank), lambda i, half: (0, 0)),
            ],
            out_specs=[
                pl.BlockSpec(memory_space=pltpu.VMEM),
                pl.BlockSpec((tile, rank), lambda i, half: (i, 0)),
            ],
        ),
        out_shape=[pltpu.VMEM((count, cols), BF16), jax.ShapeDtypeStruct((count, rank), F32)],
        compiler_params=pltpu.CompilerParams(vmem_limit_bytes=24 * MIB),
        cost_estimate=pl.CostEstimate(
            flops=2 * count * cols * rank, bytes_accessed=4 * count * cols, transcendentals=0
        ),
        name="left_product",
    )(half, grad, error, init)


def right_kernel(order_ref, near_ref, far_ref, left_near_ref, left_far_ref, out_ref, lhs_ref):
    units = out_ref.shape[0] // order_ref.shape[0]
    count = near_ref.shape[0]
    lhs_ref[:, :count] = left_near_ref[...].T.astype(BF16)
    lhs_ref[:, count:] = left_far_ref[...].T.astype(BF16)

    @pl.loop(0, order_ref.shape[0])
    def _(block):
        start = order_ref[block] * (units * LANES)
        for first in range(0, units, 2):
            width = min(2, units - first)
            cols = pl.ds(pl.multiple_of(start + first * LANES, LANES), width * LANES)
            product = jnp.dot(lhs_ref[:, :count], near_ref[:, cols], preferred_element_type=F32)
            product += jnp.dot(lhs_ref[:, count:], far_ref[:, cols], preferred_element_type=F32)
            for unit in range(width):
                out_ref[block * units + first + unit] = product[
                    :, unit * LANES : (unit + 1) * LANES
                ].astype(out_ref.dtype)


def right_product(order, near, far, left_near, left_far, units, dtype):
    count, cols = near.shape
    rank = left_near.shape[1]
    vmem = pl.BlockSpec(memory_space=pltpu.VMEM)
    total = order.shape[0] * units
    return pl.pallas_call(
        right_kernel,
        grid_spec=pltpu.PrefetchScalarGridSpec(
            num_scalar_prefetch=1,
            grid=(),
            in_specs=[vmem] * 4,
            out_specs=vmem,
            scratch_shapes=[pltpu.VMEM((rank, 2 * count), BF16)],
        ),
        out_shape=jax.ShapeDtypeStruct((total, rank, LANES), dtype),
        compiler_params=pltpu.CompilerParams(vmem_limit_bytes=24 * MIB),
        cost_estimate=pl.CostEstimate(
            flops=4 * count * total * LANES * rank, bytes_accessed=4 * MIB, transcendentals=0
        ),
        name="right_product",
    )(order, in_vmem(near), in_vmem(far), left_near, left_far)


def in_vmem(x):
    return pltpu.with_memory_space_constraint(x, pltpu.VMEM)


def error_kernel(order_ref, halves_ref, near_ref, far_ref, base_near_ref, base_far_ref, right_ref, *rest):
    del halves_ref
    out_ref = rest[-1]
    units = right_ref.shape[0]
    start = order_ref[pl.program_id(0)] * (units * LANES)

    def write(comp_ref, base_ref):
        for first in range(0, units, 2):
            width = min(2, units - first)
            right = right_ref[first]
            if width == 2:
                right = jnp.concatenate([right, right_ref[first + 1]], axis=1)
            cols = pl.ds(pl.multiple_of(start + first * LANES, LANES), width * LANES)
            product = jnp.dot(base_ref[...], right, preferred_element_type=F32)
            out_ref[:, first * LANES : (first + width) * LANES] = (
                comp_ref[:, cols].astype(F32) - product
            ).astype(BF16)

    @pl.when(pl.program_id(1) == 0)
    def _():
        write(near_ref, base_near_ref)

    @pl.when(pl.program_id(1) == 1)
    def _():
        write(far_ref, base_far_ref)


def new_error(order, halves, near, far, base_near, base_far, right, units, held=None):
    count, cols = near.shape
    rank = base_near.shape[1]
    vmem = pl.BlockSpec(memory_space=pltpu.VMEM)
    blocks = order.shape[0]
    extra = [] if held is None else [held]
    return pl.pallas_call(
        error_kernel,
        grid_spec=pltpu.PrefetchScalarGridSpec(
            num_scalar_prefetch=2,
            grid=(blocks, 2),
            in_specs=[vmem] * 4
            + [pl.BlockSpec((units, rank, LANES), lambda j, h, order, halves: (j, 0, 0))]
            + [pl.BlockSpec(memory_space=pl.ANY)] * len(extra),
            out_specs=pl.BlockSpec(
                (count, units * LANES), lambda j, h, order, halves: (halves[h], order[j])
            ),
        ),
        out_shape=jax.ShapeDtypeStruct((2 * count, cols), BF16),
        input_output_aliases={7: 0} if extra else {},
        compiler_params=pltpu.CompilerParams(vmem_limit_bytes=24 * MIB),
        cost_estimate=pl.CostEstimate(
            flops=4 * count * blocks * units * LANES * rank,
            bytes_accessed=4 * count * blocks * units * LANES,
            transcendentals=0,
        ),
        name="new_error",
    )(order, halves, in_vmem(near), in_vmem(far), base_near, base_far, right, *extra)


class Exchange:
    def __init__(self, dp, mp):
        self.dp, self.mp = dp, mp
        mp_bits = [("mp", 1 << k) for k in range(mp.bit_length() - 1)]
        z_bits = [("dp", 2 << k) for k in range(dp.bit_length() - 2)]
        low, high = mp_bits[0], mp_bits[len(mp_bits) // 2]
        other = [bit for bit in mp_bits if bit not in (low, high)]
        self.scatter = [(low, high), (high, low)]
        rest = other + z_bits
        self.rest = list(zip(rest, rest[::-1]))
        self.replicas = list(zip(z_bits, z_bits[::-1]))
        self.other = other
        self.low, self.high = low[1], high[1]

    def send(self, x, step):
        pairs = []
        for d in range(self.dp):
            for m in range(self.mp):
                axis, bit = step[d % 2]
                to = (d ^ bit) * self.mp + m if axis == "dp" else d * self.mp + (m ^ bit)
                pairs.append((d * self.mp + m, to))
        return lax.ppermute(x, AXES, pairs)

    def core(self, x):
        return self.send(x, (("dp", 1), ("dp", 1)))

    def both_sum(self, x, step):
        sent, own = as_bf16(x)
        return own + self.send(sent, step).astype(F32)


def split3(x):
    high = lax.reduce_precision(x, 8, 7)
    mid = lax.reduce_precision(x - high, 8, 7)
    low = x - high - mid
    return jnp.stack([high, mid, low]).astype(BF16)


def join3(parts):
    parts = parts.astype(F32)
    return parts[0] + (parts[1] + parts[2])


def gram_of(block):
    return lax.dot_general(
        block, block, (((0,), (0,)), ((), ())), precision=lax.Precision.HIGHEST, preferred_element_type=F32
    )


def on_device(dp, mp, grad, error, init):
    grad, error = grad[0], error[0]
    rows, cols = grad.shape
    rank = init.shape[1]
    net = Exchange(dp, mp)
    units = cols // 8 // LANES

    d = lax.axis_index("dp").astype(jnp.int32)
    m = lax.axis_index("mp").astype(jnp.int32)
    core = d % 2
    low = (m & net.low) // net.low
    high = (m & net.high) // net.high

    def blocks_of(which_core):
        out = []
        for a in range(2):
            for b in range(2):
                flip_low = jnp.where(which_core == 0, a, b)
                flip_high = jnp.where(which_core == 0, b, a)
                out.append((high ^ flip_high) * 4 + (low ^ flip_low) * 2 + which_core)
        return jnp.stack(out).astype(jnp.int32)

    order_near, order_far = blocks_of(core), blocks_of(1 - core)
    halves = jnp.stack([core, 1 - core])

    comp_far, left_far = left_product(halves[1:], grad, error, init)
    arrived = net.core(left_far)
    comp_near, left_near = left_product(halves[:1], grad, error, init)
    left_near = left_near + arrived
    for step in net.replicas:
        left_near = net.both_sum(left_near, step)
    left_far = net.core(left_near)

    gram = gram_of(left_near) + gram_of(left_far)

    part_far = right_product(order_far, comp_near, comp_far, left_near, left_far, units, BF16)
    arrived = net.core(part_far)
    part = right_product(order_near, comp_near, comp_far, left_near, left_far, units, F32)
    part = part + arrived.astype(F32)

    for step in net.scatter:
        kept = part.shape[0] // 2
        sent = jnp.concatenate([part[kept:].astype(BF16), split3(gram)], axis=0)
        arrived = net.send(sent, step)
        part = part[:kept] + arrived[:kept].astype(F32)
        gram = gram + join3(arrived[kept:])
    for bit in net.other:
        gram = gram + net.send(gram, (bit, bit))

    lower = jnp.linalg.cholesky(gram)
    inverse = jax.scipy.linalg.solve_triangular(lower, jnp.eye(rank, dtype=F32), lower=True)

    first, later = net.rest[0], net.rest[1:]
    d_bit = jnp.where(core == 0, d & first[0][1] if first[0][0] == "dp" else m & first[0][1],
                      d & first[1][1] if first[1][0] == "dp" else m & first[1][1])
    upper = d_bit != 0
    top, bottom = part[:, : rank // 2], part[:, rank // 2 :]
    arrived = net.send(jnp.where(upper, top, bottom).astype(BF16), first)
    part = jnp.where(upper, bottom, top) + arrived.astype(F32)
    for step in later:
        part = net.both_sum(part, step)
    sent, own = as_bf16(part)
    arrived = net.send(sent, first)
    summed = jnp.where(
        upper, jnp.concatenate([arrived, sent], axis=1), jnp.concatenate([sent, arrived], axis=1)
    ).astype(F32)

    right = lax.dot_general(
        summed, inverse, (((1,), (1,)), ((), ())), precision=lax.Precision.HIGHEST, preferred_element_type=F32
    )
    right = (jnp.swapaxes(right, 1, 2) / dp).astype(BF16)

    def base_of(left):
        return lax.dot_general(
            left, inverse, (((1,), (1,)), ((), ())), precision=lax.Precision.HIGHEST, preferred_element_type=F32
        ).astype(BF16)

    base_near, base_far = base_of(left_near), base_of(left_far)

    for step in net.scatter[::-1]:
        right = jnp.concatenate([right, net.send(right, step)], axis=0)
    right_far = net.core(right)
    write = functools.partial(new_error, halves=halves, near=comp_near, far=comp_far,
                              base_near=base_near, base_far=base_far, units=units)
    out = write(order_near, right=right)
    out = write(order_far, right=right_far, held=out)

    share = cols // mp
    width = units * LANES
    covered = max(share, width)
    everything = jnp.concatenate([right, right_far], axis=0)
    names = jnp.concatenate([order_near, order_far])
    first_block = m * share // width
    picks = [
        lax.dynamic_slice_in_dim(everything, jnp.argmax(names == first_block + k) * units, units, 0)
        for k in range(covered // width)
    ]
    chosen = jnp.swapaxes(jnp.concatenate(picks, axis=0), 1, 2).reshape(covered, rank)
    right_factor = lax.dynamic_slice_in_dim(chosen, m * share - first_block * width, share, 0)
    return (out[None], right_factor)


def solution(mesh):
    return jax.shard_map(
        functools.partial(on_device, mesh.shape["dp"], mesh.shape["mp"]),
        mesh=mesh,
        in_specs=(P("dp", "mp", None), P("dp", "mp", None), P()),
        out_specs=(P("dp", "mp", None), P("mp", None)),
        check_vma=False,
    )
```

```python
import functools

import jax
import jax.numpy as jnp
import numpy as np
from jax import lax
from jax.experimental import pallas as pl
from jax.experimental.pallas import tpu as pltpu
from jax.sharding import PartitionSpec as P

F32 = jnp.float32
BF16 = jnp.bfloat16
LANES = 128
MIB = 1024 * 1024
AXES = ("dp", "mp")
PIECES = 14
LEAF = 8

VMEM = pl.BlockSpec(memory_space=pltpu.VMEM)
HBM = pl.BlockSpec(memory_space=pltpu.HBM)
SMEM = pl.BlockSpec(memory_space=pltpu.SMEM)

HALF, NEAR, FAR, UPPER, WIDTH = 0, 2, 6, 10, 16


def call(kernel, name, outs, ins, vmem_mib, micros, **more):
    return pl.pallas_call(
        kernel,
        out_shape=outs,
        in_specs=ins,
        compiler_params=pltpu.CompilerParams(vmem_limit_bytes=vmem_mib * MIB),
        cost_estimate=pl.CostEstimate(flops=0, bytes_accessed=int(micros * 3.5e6), transcendentals=0),
        name=name,
        **more,
    )


def shaped(shape, dtype):
    return jax.ShapeDtypeStruct(shape, dtype)


def in_hbm(x):
    return pltpu.with_memory_space_constraint(x, pltpu.HBM)


def in_vmem(x):
    return pltpu.with_memory_space_constraint(x, pltpu.VMEM)


def left_kernel(pieces, table, grad, error, init, comp, near, far, error_v, init_v, sems):
    rows, cols = comp.shape
    count, width = rows // 2, cols // pieces

    def copies(i):
        at = pl.ds(i * width, width)
        out = [pltpu.make_async_copy(init.at[at], init_v.at[at], sems.at[4, i])]
        for half in range(2):
            source = pl.ds(pl.multiple_of(table[HALF + half] * count, count), count)
            target = pl.ds(half * count, count)
            out.append(pltpu.make_async_copy(grad.at[source, at], comp.at[target, at], sems.at[half, i]))
            out.append(pltpu.make_async_copy(error.at[source, at], error_v.at[target, at], sems.at[2 + half, i]))
        return out

    for i in range(pieces):
        for copy in copies(i):
            copy.start()
    for i in range(pieces):
        for copy in copies(i):
            copy.wait()
        at = pl.ds(i * width, width)
        total = (comp[:, at].astype(F32) + error_v[:, at].astype(F32)).astype(BF16)
        comp[:, at] = total
        part = lax.dot_general(init_v[at].T, total, (((1,), (1,)), ((), ())), preferred_element_type=F32)
        if i == 0:
            near[...] = part[:, :count]
            far[...] = part[:, count:]
        else:
            near[...] += part[:, :count]
            far[...] += part[:, count:]


def left_product(table, grad, error, init):
    rows, cols = grad.shape
    rank = init.shape[1]
    return call(
        functools.partial(left_kernel, PIECES),
        "left_product",
        [pltpu.VMEM((rows, cols), BF16), shaped((rank, rows // 2), F32), shaped((rank, rows // 2), F32)],
        [SMEM, HBM, HBM, HBM],
        26,
        12,
        out_specs=[VMEM] * 3,
        scratch_shapes=[
            pltpu.VMEM((rows, cols), BF16),
            pltpu.VMEM((cols, rank), BF16),
            pltpu.SemaphoreType.DMA((5, PIECES)),
        ],
    )(table, in_hbm(grad), in_hbm(error), in_hbm(init))


def right_kernel(units, first, table, comp, near, far, out):
    rows = comp.shape[0]
    count = rows // 2

    @pl.loop(0, out.shape[0] // units)
    def _(block):
        start = table[first + block] * (units * LANES)
        for unit in range(0, units, 2):
            wide = min(2, units - unit)
            at = pl.ds(pl.multiple_of(start + unit * LANES, LANES), wide * LANES)
            product = jnp.dot(near[...], comp[:count, at], preferred_element_type=F32)
            product += jnp.dot(far[...], comp[count:, at], preferred_element_type=F32)
            for k in range(wide):
                out[block * units + unit + k] = product[:, k * LANES : (k + 1) * LANES].astype(out.dtype)


def right_product(table, first, blocks, units, comp, near, far, dtype):
    rank = near.shape[0]
    return call(
        functools.partial(right_kernel, units, first),
        "right_product",
        shaped((blocks * units, rank, LANES), dtype),
        [SMEM, VMEM, VMEM, VMEM],
        4,
        0.7 * blocks,
        out_specs=VMEM,
    )(table, in_vmem(comp), near, far)


def new_error_kernel(units, blocks, table, comp, near, far, *rest):
    arrays = rest[: 1 + max(which for _, which, _ in blocks)]
    out, buf, sems = rest[-3:]
    count = comp.shape[0] // 2
    width = units * LANES
    copies = []
    for j, (entry, which, place) in enumerate(blocks):
        right = arrays[which]
        start = pl.multiple_of(table[entry] * width, LANES)
        for half, base in enumerate((near, far)):
            for unit in range(0, units, 2):
                wide = min(2, units - unit)
                factor = [right[place * units + unit + k] for k in range(wide)]
                factor = jnp.concatenate(factor, axis=1) if wide > 1 else factor[0]
                product = jnp.dot(base[...], factor, preferred_element_type=F32)
                at = pl.ds(pl.multiple_of(start + unit * LANES, LANES), wide * LANES)
                kept = comp[half * count : (half + 1) * count, at].astype(F32)
                buf[half, j, :, unit * LANES : (unit + wide) * LANES] = (kept - product).astype(BF16)
            rows = pl.ds(pl.multiple_of(table[HALF + half] * count, count), count)
            copy = pltpu.make_async_copy(buf.at[half, j], out.at[rows, pl.ds(start, width)], sems.at[half, j])
            copy.start()
            copies.append(copy)
    for copy in copies:
        copy.wait()


def new_error(table, blocks, arrays, units, comp, near, far, held=None):
    rows, cols = comp.shape
    extra = [] if held is None else [in_hbm(held)]
    return call(
        functools.partial(new_error_kernel, units, blocks),
        "new_error",
        shaped((rows, cols), BF16),
        [SMEM] + [VMEM] * (3 + len(arrays)) + [HBM] * len(extra),
        12,
        1 + 0.7 * len(blocks),
        out_specs=HBM,
        scratch_shapes=[
            pltpu.VMEM((2, len(blocks), rows // 2, units * LANES), BF16),
            pltpu.SemaphoreType.DMA((2, len(blocks))),
        ],
        input_output_aliases={4 + len(arrays): 0} if extra else {},
    )(table, in_vmem(comp), near, far, *arrays, *extra)


def leaf_steps(state, leaf):
    n, b = state.shape[0], LEAF
    base = leaf * b

    def splat(v):
        return jnp.broadcast_to(v, (b, n))

    def column(tile, j):
        return splat(state[b * tile : b * tile + b, base + j : base + j + 1])

    here = [column(leaf, j) for j in range(b)]
    a = [[splat(here[j][i : i + 1]) if j <= i else None for j in range(b)] for i in range(b)]
    mult = [[None] * b for _ in range(b)]
    unit = [[None] * b for _ in range(b)]
    recip, scale = [], []
    for k in range(b):
        recip.append(1.0 / a[k][k])
        scale.append(lax.rsqrt(a[k][k]))
        for i in range(k + 1, b):
            mult[i][k] = a[i][k] * recip[k]
        for i in range(k + 1, b):
            for j in range(k + 1, i + 1):
                a[i][j] = a[i][j] - mult[i][k] * a[j][k]
    for j in range(b):
        for i in range(j + 1, b):
            total = mult[i][j]
            for k in range(j + 1, i):
                total = total + mult[i][k] * unit[k][j]
            unit[i][j] = -total
    rows_x = [splat(state[base + j : base + j + 1, n:]) for j in range(b)]
    if leaf + 1 < n // b:
        rows_g = [splat(state[base + j : base + j + 1, :n]) for j in range(b)]

        def term(k, j):
            return recip[k] if j == k else recip[k] * unit[k][j]

        inverse = [[None] * b for _ in range(b)]
        for i in range(b):
            for j in range(i + 1):
                total = term(i, j)
                for k in range(i + 1, b):
                    total = total + unit[k][i] * term(k, j)
                inverse[i][j] = inverse[j][i] = total

        def mixed(rows):
            out = []
            for k in range(b):
                total = inverse[k][0] * rows[0]
                for j in range(1, b):
                    total = total + inverse[k][j] * rows[j]
                out.append(total)
            return out

        mixed_g, mixed_x = mixed(rows_g), mixed(rows_x)
        for tile in range(leaf + 1, n // b):
            at = slice(b * tile, b * tile + b)
            columns = [column(tile, j) for j in range(b)]
            g, x = state[at, :n], state[at, n:]
            for k in range(b):
                g = g - columns[k] * mixed_g[k]
                x = x - columns[k] * mixed_x[k]
            state[at, :n] = g
            state[at, n:] = x
    for i in range(b):
        total = rows_x[i]
        for j in range(i):
            total = total + unit[i][j] * rows_x[j]
        state[base + i : base + i + 1, n:] = (total * scale[i])[:1]


def leaves_kernel(leaves, source, state):
    n = state.shape[0]
    if source.shape == state.shape:
        state[...] = source[...]
    else:
        state[:, :n] = source[...]
        row = lax.broadcasted_iota(jnp.int32, (n, n), 0)
        state[:, n:] = (row == lax.broadcasted_iota(jnp.int32, (n, n), 1)).astype(F32)
    for leaf in leaves:
        leaf_steps(state, leaf)


def inverse_part(source, leaves):
    n = source.shape[0]
    return call(
        functools.partial(leaves_kernel, leaves),
        "inverse_part",
        shaped((n, 2 * n), F32),
        [VMEM],
        4,
        1.5,
        out_specs=VMEM,
    )(source)


def split2(x):
    high = x.astype(BF16)
    return high, (x - high.astype(F32)).astype(BF16)


def put3(ref, at, x):
    high, rest = split2(x)
    ref[at] = high
    rest = x - high.astype(F32)
    mid, low = split2(rest)
    ref[at + 1] = mid
    ref[at + 2] = low


def get3(ref, at):
    return ref[at].astype(F32) + (ref[at + 1].astype(F32) + ref[at + 2].astype(F32))


def first_kernel(part, arrived, near, far, out, gram):
    count = part.shape[0]
    contract = (((1,), (1,)), ((), ()))
    total = lax.dot_general(near[...], near[...], contract, preferred_element_type=F32)
    total += lax.dot_general(far[...], far[...], contract, preferred_element_type=F32)
    gram[...] = total
    put3(out, count, total)

    @pl.loop(0, count)
    def _(i):
        out[i] = (part[i] + arrived[i].astype(F32)).astype(BF16)


def second_kernel(part, across, arrived, gram_in, out, kept, gram):
    units = kept.shape[0]
    total = gram_in[...] + get3(arrived, 2 * units)
    gram[...] = total
    put3(out, units, total)

    @pl.loop(0, units)
    def _(i):
        j = i + units
        out[i] = (part[j] + across[j].astype(F32) + arrived[j].astype(F32)).astype(BF16)
        kept[i] = part[i] + across[i].astype(F32) + arrived[i].astype(F32)


def third_kernel(table, part, arrived, gram_in, out, kept, gram, held):
    units, rank = part.shape[:2]
    half = rank // 2
    gram[...] = gram_in[...] + get3(arrived, units)
    mine = pl.multiple_of(table[UPPER] * half, half)

    @pl.loop(0, units)
    def _(i):
        held[...] = part[i] + arrived[i].astype(F32)
        out[i] = held[pl.ds(half - mine, half), :].astype(BF16)
        kept[i] = held[pl.ds(mine, half), :]


def add_kernel(kept, arrived, out):
    @pl.loop(0, kept.shape[0])
    def _(i):
        out[i] = (kept[i].astype(F32) + arrived[i].astype(F32)).astype(BF16)


def factor_kernel(replicas, table, own, arrived, state, out, held):
    units, half = own.shape[:2]
    rank = 2 * half
    mine = pl.multiple_of(table[UPPER] * half, half)
    lhs = jnp.concatenate(split2(state[:, rank:]), axis=0)
    for i in range(units):
        at = slice(i * LANES, (i + 1) * LANES)
        held[pl.ds(mine, half), at] = own[i]
        held[pl.ds(half - mine, half), at] = arrived[i]
    for i in range(0, units, 2):
        wide = min(2, units - i)
        product = jnp.dot(lhs, held[:, i * LANES : (i + wide) * LANES], preferred_element_type=F32)
        product = (product[:rank] + product[rank:]) / replicas
        for k in range(wide):
            out[i + k] = product[:, k * LANES : (k + 1) * LANES].astype(BF16)


def base_kernel(near, far, state, near_out, far_out):
    rank = near.shape[0]
    lhs = jnp.concatenate(split2(state[:, rank:]), axis=0)
    for source, out in ((near, near_out), (far, far_out)):
        product = jnp.dot(lhs, source[...], preferred_element_type=F32)
        out[...] = (product[:rank] + product[rank:]).T.astype(BF16)


def rows_kernel(units, table, own, other, out):
    for half, source in enumerate((own, other)):
        start = table[HALF + half] * (units * LANES)

        @pl.loop(0, units)
        def _(i):
            out[pl.ds(pl.multiple_of(start + i * LANES, LANES), LANES), :] = source[i].T


class Exchange:
    def __init__(self, dp, mp):
        self.dp, self.mp = dp, mp
        mp_bits = [("mp", 1 << k) for k in range(mp.bit_length() - 1)]
        z_bits = [("dp", 2 << k) for k in range(dp.bit_length() - 2)]
        low, high = mp_bits[0], mp_bits[len(mp_bits) // 2]
        self.other = [bit for bit in mp_bits if bit not in (low, high)]
        self.scatter = [(low, high), (high, low)]
        rest = self.other + z_bits
        self.rest = list(zip(rest, rest[::-1]))
        self.replicas = list(zip(z_bits, z_bits[::-1]))
        self.low, self.high = low[1], high[1]

    def send(self, x, step):
        pairs = []
        for d in range(self.dp):
            for m in range(self.mp):
                axis, bit = step[d % 2]
                to = (d ^ bit) * self.mp + m if axis == "dp" else d * self.mp + (m ^ bit)
                pairs.append((d * self.mp + m, to))
        return lax.ppermute(x, AXES, pairs)

    def core(self, x):
        return self.send(x, (("dp", 1), ("dp", 1)))

    def tables(self):
        table = np.zeros((self.dp, self.mp, WIDTH), np.int32)
        for d in range(self.dp):
            for m in range(self.mp):
                core = d % 2
                table[d, m, HALF : HALF + 2] = core, 1 - core
                for entry, which in ((NEAR, core), (FAR, 1 - core)):
                    for k in range(4):
                        first, second = self.scatter[0][which][1], self.scatter[1][which][1]
                        at = m ^ (first * (k // 2)) ^ (second * (k % 2))
                        low, high = int(at & self.low != 0), int(at & self.high != 0)
                        table[d, m, entry + k] = high * 4 + low * 2 + which
                axis, bit = self.rest[0][core]
                table[d, m, UPPER] = int((d if axis == "dp" else m) & bit != 0)
        return table


def on_device(dp, mp, grad, error, init, table):
    grad, error, table = grad[0], error[0], table.reshape(-1)
    rows, cols = grad.shape
    rank = init.shape[1]
    half = rank // 2
    net = Exchange(dp, mp)
    units = cols // 8 // LANES
    square = (rank, LANES)

    comp, near, far = left_product(table, grad, error, init)
    near = near + net.core(far)
    for step in net.replicas:
        sent = lax.reduce_precision(near, 8, 7)
        near = sent + net.send(sent.astype(BF16), step).astype(F32)
    near = near.astype(BF16)
    far = net.core(near)

    def right(first, dtype):
        return right_product(table, first, 2, units, comp, near, far, dtype)

    across = net.core(right(FAR + 2, BF16))
    part = right(NEAR + 2, F32)
    sent, gram = call(
        first_kernel, "first_sum",
        [shaped((2 * units + 3, *square), BF16), shaped((rank, rank), F32)],
        [VMEM] * 4, 4, 0.5, out_specs=[VMEM] * 2,
    )(part, across, near, far)
    arrived = net.send(sent, net.scatter[0])
    across = net.core(right(FAR, BF16))
    part = right(NEAR, F32)
    sent, kept, gram = call(
        second_kernel, "second_sum",
        [shaped((units + 3, *square), BF16), shaped((units, *square), F32), shaped((rank, rank), F32)],
        [VMEM] * 4, 4, 0.5, out_specs=[VMEM] * 3,
    )(part, across, arrived, gram)
    arrived = net.send(sent, net.scatter[1])
    sent, kept, gram = call(
        third_kernel, "third_sum",
        [shaped((units, half, LANES), BF16), shaped((units, half, LANES), F32), shaped((rank, rank), F32)],
        [SMEM] + [VMEM] * 3, 4, 0.5, out_specs=[VMEM] * 3,
        scratch_shapes=[pltpu.VMEM(square, F32)],
    )(table, kept, arrived, gram)
    for bit in net.other:
        gram = gram + net.send(gram, (bit, bit))

    leaves = list(range(rank // LEAF))
    state = gram
    for k in range(3):
        state = inverse_part(state, leaves[len(leaves) * k // 3 : len(leaves) * (k + 1) // 3])
    for step in net.rest:
        kept = call(
            add_kernel, "pair_sum", shaped((units, half, LANES), BF16), [VMEM] * 2, 2, 0.3, out_specs=VMEM
        )(kept, net.send(sent, step))
        sent = kept
    own = call(
        functools.partial(factor_kernel, dp), "factor", shaped((units, *square), BF16),
        [SMEM] + [VMEM] * 3, 4, 0.7, out_specs=VMEM,
        scratch_shapes=[pltpu.VMEM((rank, units * LANES), BF16)],
    )(table, sent, net.send(sent, net.rest[0]), state)
    base_near, base_far = call(
        base_kernel, "base", [shaped((rows // 2, rank), BF16)] * 2, [VMEM] * 3, 4, 0.7, out_specs=[VMEM] * 2
    )(near, far, state)

    write = functools.partial(new_error, table, units=units, comp=comp, near=base_near, far=base_far)
    own = jnp.concatenate([own, net.send(own, net.scatter[1])], axis=0)
    arrived = net.send(own, net.scatter[0])
    other = net.core(own)
    out = write([(NEAR, 0, 0), (NEAR + 1, 0, 1)], [own])
    crossed = net.core(arrived)
    out = write(
        [(FAR, 0, 0), (FAR + 1, 0, 1), (NEAR + 2, 1, 0), (NEAR + 3, 1, 1)], [other, arrived], held=out
    )
    out = write([(FAR + 2, 0, 0), (FAR + 3, 0, 1)], [crossed], held=out)

    share, width = cols // mp, units * LANES
    if share == 2 * width:
        right_factor = call(
            functools.partial(rows_kernel, units), "factor_rows", shaped((share, rank), BF16),
            [SMEM, VMEM, VMEM], 4, 1, out_specs=VMEM,
        )(table, own, other)
    else:
        everything = jnp.concatenate([own, arrived, other, crossed], axis=0)
        block = lax.axis_index("mp") * share // width
        place = jnp.argmax(table[NEAR : NEAR + 8] == block)
        chosen = lax.dynamic_slice_in_dim(everything, place * units, units, 0)
        chosen = jnp.swapaxes(chosen, 1, 2).reshape(width, rank)
        right_factor = lax.dynamic_slice_in_dim(chosen, lax.axis_index("mp") * share - block * width, share, 0)
    return (out[None], right_factor)


def solution(mesh):
    dp, mp = mesh.shape["dp"], mesh.shape["mp"]
    table = Exchange(dp, mp).tables()
    run = jax.shard_map(
        functools.partial(on_device, dp, mp),
        mesh=mesh,
        in_specs=(P("dp", "mp", None), P("dp", "mp", None), P(), P("dp", "mp", None)),
        out_specs=(P("dp", "mp", None), P("mp", None)),
        check_vma=False,
    )

    def whole(grad, error, init_factor):
        return run(grad, error, init_factor, jnp.asarray(table))

    return whole
```

```python
import functools

import jax
import jax.numpy as jnp
from jax import lax
from jax.experimental import pallas as pl
from jax.experimental.pallas import tpu as pltpu
from jax.sharding import PartitionSpec as P

F32 = jnp.float32
BF16 = jnp.bfloat16
LANES = 128
MIB = 1024 * 1024
AXES = ("dp", "mp")
PIECES = 14
LEAF = 8

VMEM = pl.BlockSpec(memory_space=pltpu.VMEM)
HBM = pl.BlockSpec(memory_space=pltpu.HBM)
SMEM = pl.BlockSpec(memory_space=pltpu.SMEM)

NEAR, FAR = 0, 1


class Place:
    def __init__(self, net, place):
        self.net = net
        self.dp, self.mp = place[0][0], place[1][0]
        self.core = self.dp & 1

    def half(self, side):
        return self.core if side == NEAR else 1 - self.core

    def bit(self, name):
        axis, value = name
        return ((self.dp if axis == "dp" else self.mp) >> (value.bit_length() - 1)) & 1

    def block(self, side, k):
        core = self.half(side)
        a, b = k // 2, k % 2
        low = self.bit(self.net.low) ^ (a + (b - a) * core)
        high = self.bit(self.net.high) ^ (b + (a - b) * core)
        return high * 4 + low * 2 + core

    def upper(self):
        first, second = (self.bit(name) for name in self.net.rest[0])
        return first + (second - first) * self.core


def call(kernel, name, outs, ins, vmem_mib, micros, **more):
    return pl.pallas_call(
        kernel,
        out_shape=outs,
        in_specs=ins,
        compiler_params=pltpu.CompilerParams(vmem_limit_bytes=vmem_mib * MIB),
        cost_estimate=pl.CostEstimate(flops=0, bytes_accessed=int(micros * 3.5e6), transcendentals=0),
        name=name,
        **more,
    )


def shaped(shape, dtype):
    return jax.ShapeDtypeStruct(shape, dtype)


def in_hbm(x):
    return pltpu.with_memory_space_constraint(x, pltpu.HBM)


def in_vmem(x):
    return pltpu.with_memory_space_constraint(x, pltpu.VMEM)


def left_kernel(net, pieces, dp, mp, grad, error, init, comp, near, far, error_v, init_v, sems):
    place = Place(net, (dp, mp))
    rows, cols = comp.shape
    count, width = rows // 2, cols // pieces

    def copies(i):
        at = pl.ds(i * width, width)
        out = [pltpu.make_async_copy(init.at[at], init_v.at[at], sems.at[4, i])]
        for half in range(2):
            source = pl.ds(pl.multiple_of(place.half(half) * count, count), count)
            target = pl.ds(half * count, count)
            out.append(pltpu.make_async_copy(grad.at[source, at], comp.at[target, at], sems.at[half, i]))
            out.append(pltpu.make_async_copy(error.at[source, at], error_v.at[target, at], sems.at[2 + half, i]))
        return out

    for i in range(pieces):
        for copy in copies(i):
            copy.start()
    for i in range(pieces):
        for copy in copies(i):
            copy.wait()
        at = pl.ds(i * width, width)
        total = (comp[:, at].astype(F32) + error_v[:, at].astype(F32)).astype(BF16)
        comp[:, at] = total
        part = lax.dot_general(init_v[at].T, total, (((1,), (1,)), ((), ())), preferred_element_type=F32)
        if i == 0:
            near[...] = part[:, :count]
            far[...] = part[:, count:]
        else:
            near[...] += part[:, :count]
            far[...] += part[:, count:]


def left_product(net, place, grad, error, init):
    rows, cols = grad.shape
    rank = init.shape[1]
    return call(
        functools.partial(left_kernel, net, PIECES),
        "left_product",
        [pltpu.VMEM((rows, cols), BF16), shaped((rank, rows // 2), F32), shaped((rank, rows // 2), F32)],
        [SMEM, SMEM, HBM, HBM, HBM],
        26,
        12,
        out_specs=[VMEM] * 3,
        scratch_shapes=[
            pltpu.VMEM((rows, cols), BF16),
            pltpu.VMEM((cols, rank), BF16),
            pltpu.SemaphoreType.DMA((5, PIECES)),
        ],
    )(*place, in_hbm(grad), in_hbm(error), in_hbm(init))


def right_kernel(net, units, side, places, dp, mp, comp, near, far, out):
    place = Place(net, (dp, mp))
    rows = comp.shape[0]
    count = rows // 2
    for block, k in enumerate(places):
        start = place.block(side, k) * (units * LANES)
        for unit in range(0, units, 2):
            wide = min(2, units - unit)
            at = pl.ds(pl.multiple_of(start + unit * LANES, LANES), wide * LANES)
            product = jnp.dot(near[...], comp[:count, at], preferred_element_type=F32)
            product += jnp.dot(far[...], comp[count:, at], preferred_element_type=F32)
            for k in range(wide):
                out[block * units + unit + k] = product[:, k * LANES : (k + 1) * LANES].astype(out.dtype)


def right_product(net, place, side, places, units, comp, near, far, dtype):
    rank = near.shape[0]
    return call(
        functools.partial(right_kernel, net, units, side, places),
        "right_product",
        shaped((len(places) * units, rank, LANES), dtype),
        [SMEM, SMEM, VMEM, VMEM, VMEM],
        4,
        0.7 * len(places),
        out_specs=VMEM,
    )(*place, in_vmem(comp), near, far)


def new_error_kernel(net, units, side, places, dp, mp, comp, near, far, right, *rest):
    place = Place(net, (dp, mp))
    out, buf, sems = rest[-3:]
    count = comp.shape[0] // 2
    width = units * LANES
    copies = []
    for j, k in enumerate(places):
        start = pl.multiple_of(place.block(side, k) * width, LANES)
        for half, base in enumerate((near, far)):
            for unit in range(0, units, 2):
                wide = min(2, units - unit)
                factor = [right[j * units + unit + i] for i in range(wide)]
                factor = jnp.concatenate(factor, axis=1) if wide > 1 else factor[0]
                product = jnp.dot(base[...], factor, preferred_element_type=F32)
                at = pl.ds(pl.multiple_of(start + unit * LANES, LANES), wide * LANES)
                kept = comp[half * count : (half + 1) * count, at].astype(F32)
                buf[half, j, :, unit * LANES : (unit + wide) * LANES] = (kept - product).astype(BF16)
            rows = pl.ds(pl.multiple_of(place.half(half) * count, count), count)
            copy = pltpu.make_async_copy(buf.at[half, j], out.at[rows, pl.ds(start, width)], sems.at[half, j])
            copy.start()
            copies.append(copy)
    for copy in copies:
        copy.wait()


def new_error(net, place, side, places, right, units, comp, near, far, held=None):
    rows, cols = comp.shape
    extra = [] if held is None else [in_hbm(held)]
    return call(
        functools.partial(new_error_kernel, net, units, side, places),
        "new_error",
        shaped((rows, cols), BF16),
        [SMEM] * 2 + [VMEM] * 4 + [HBM] * len(extra),
        12,
        1 + 0.7 * len(places),
        out_specs=HBM,
        scratch_shapes=[
            pltpu.VMEM((2, len(places), rows // 2, units * LANES), BF16),
            pltpu.SemaphoreType.DMA((2, len(places))),
        ],
        input_output_aliases={6: 0} if extra else {},
    )(*place, in_vmem(comp), near, far, right, *extra)


def leaf_steps(state, leaf):
    n, b = state.shape[0], LEAF
    base = leaf * b

    def splat(v):
        return jnp.broadcast_to(v, (b, n))

    def column(tile, j):
        return splat(state[b * tile : b * tile + b, base + j : base + j + 1])

    here = [column(leaf, j) for j in range(b)]
    a = [[splat(here[j][i : i + 1]) if j <= i else None for j in range(b)] for i in range(b)]
    mult = [[None] * b for _ in range(b)]
    unit = [[None] * b for _ in range(b)]
    recip, scale = [], []
    for k in range(b):
        recip.append(1.0 / a[k][k])
        scale.append(lax.rsqrt(a[k][k]))
        for i in range(k + 1, b):
            mult[i][k] = a[i][k] * recip[k]
        for i in range(k + 1, b):
            for j in range(k + 1, i + 1):
                a[i][j] = a[i][j] - mult[i][k] * a[j][k]
    for j in range(b):
        for i in range(j + 1, b):
            total = mult[i][j]
            for k in range(j + 1, i):
                total = total + mult[i][k] * unit[k][j]
            unit[i][j] = -total
    rows_x = [splat(state[base + j : base + j + 1, n:]) for j in range(b)]
    if leaf + 1 < n // b:
        rows_g = [splat(state[base + j : base + j + 1, :n]) for j in range(b)]

        def term(k, j):
            return recip[k] if j == k else recip[k] * unit[k][j]

        inverse = [[None] * b for _ in range(b)]
        for i in range(b):
            for j in range(i + 1):
                total = term(i, j)
                for k in range(i + 1, b):
                    total = total + unit[k][i] * term(k, j)
                inverse[i][j] = inverse[j][i] = total

        def mixed(rows):
            out = []
            for k in range(b):
                total = inverse[k][0] * rows[0]
                for j in range(1, b):
                    total = total + inverse[k][j] * rows[j]
                out.append(total)
            return out

        mixed_g, mixed_x = mixed(rows_g), mixed(rows_x)
        for tile in range(leaf + 1, n // b):
            at = slice(b * tile, b * tile + b)
            columns = [column(tile, j) for j in range(b)]
            g, x = state[at, :n], state[at, n:]
            for k in range(b):
                g = g - columns[k] * mixed_g[k]
                x = x - columns[k] * mixed_x[k]
            state[at, :n] = g
            state[at, n:] = x
    for i in range(b):
        total = rows_x[i]
        for j in range(i):
            total = total + unit[i][j] * rows_x[j]
        state[base + i : base + i + 1, n:] = (total * scale[i])[:1]


def leaves_kernel(leaves, source, state):
    n = state.shape[0]
    if source.shape == state.shape:
        state[...] = source[...]
    else:
        state[:, :n] = source[...]
        row = lax.broadcasted_iota(jnp.int32, (n, n), 0)
        state[:, n:] = (row == lax.broadcasted_iota(jnp.int32, (n, n), 1)).astype(F32)
    for leaf in leaves:
        leaf_steps(state, leaf)


def inverse_part(source, leaves):
    n = source.shape[0]
    return call(
        functools.partial(leaves_kernel, leaves),
        "inverse_part",
        shaped((n, 2 * n), F32),
        [VMEM],
        4,
        1.5,
        out_specs=VMEM,
    )(source)


def split2(x):
    high = x.astype(BF16)
    return high, (x - high.astype(F32)).astype(BF16)


def put2(ref, at, x):
    ref[at], ref[at + 1] = split2(x)


def get2(ref, at):
    return ref[at].astype(F32) + ref[at + 1].astype(F32)


def first_kernel(part, arrived, near, far, out, gram):
    count = part.shape[0]
    contract = (((1,), (1,)), ((), ()))
    total = lax.dot_general(near[...], near[...], contract, preferred_element_type=F32)
    total += lax.dot_general(far[...], far[...], contract, preferred_element_type=F32)
    gram[...] = total
    put2(out, count, total)

    @pl.loop(0, count)
    def _(i):
        out[i] = (part[i] + arrived[i].astype(F32)).astype(BF16)


def second_kernel(part, across, arrived, gram_in, out, kept, gram):
    units = kept.shape[0]
    total = gram_in[...] + get2(arrived, 2 * units)
    gram[...] = total
    put2(out, units, total)

    @pl.loop(0, units)
    def _(i):
        j = i + units
        out[i] = (part[j] + across[j].astype(F32) + arrived[j].astype(F32)).astype(BF16)
        kept[i] = part[i] + across[i].astype(F32) + arrived[i].astype(F32)


def third_kernel(net, dp, mp, part, arrived, gram_in, out, kept, gram, held):
    units, rank = part.shape[:2]
    half = rank // 2
    gram[...] = gram_in[...] + get2(arrived, units)
    mine = pl.multiple_of(Place(net, (dp, mp)).upper() * half, half)

    @pl.loop(0, units)
    def _(i):
        held[...] = part[i] + arrived[i].astype(F32)
        out[i] = held[pl.ds(half - mine, half), :].astype(BF16)
        kept[i] = held[pl.ds(mine, half), :]


def add_kernel(kept, arrived, out):
    @pl.loop(0, kept.shape[0])
    def _(i):
        out[i] = (kept[i].astype(F32) + arrived[i].astype(F32)).astype(BF16)


def factor_kernel(net, dp, mp, own, arrived, state, out, held):
    units, half = own.shape[:2]
    rank = 2 * half
    mine = pl.multiple_of(Place(net, (dp, mp)).upper() * half, half)
    lhs = jnp.concatenate(split2(state[:, rank:]), axis=0)
    for i in range(units):
        at = slice(i * LANES, (i + 1) * LANES)
        held[pl.ds(mine, half), at] = own[i]
        held[pl.ds(half - mine, half), at] = arrived[i]
    for i in range(0, units, 2):
        wide = min(2, units - i)
        product = jnp.dot(lhs, held[:, i * LANES : (i + wide) * LANES], preferred_element_type=F32)
        product = (product[:rank] + product[rank:]) / net.dp
        for k in range(wide):
            out[i + k] = product[:, k * LANES : (k + 1) * LANES].astype(BF16)


def base_kernel(near, far, state, near_out, far_out):
    rank = near.shape[0]
    lhs = jnp.concatenate(split2(state[:, rank:]), axis=0)
    for source, out in ((near, near_out), (far, far_out)):
        product = jnp.dot(lhs, source[...], preferred_element_type=F32)
        out[...] = (product[:rank] + product[rank:]).T.astype(BF16)


def rows_kernel(net, units, dp, mp, own, other, out):
    place = Place(net, (dp, mp))
    for side, source in ((NEAR, own), (FAR, other)):
        start = place.half(side) * (units * LANES)
        for i in range(units):
            out[pl.ds(pl.multiple_of(start + i * LANES, LANES), LANES), :] = source[i].T


class Exchange:
    def __init__(self, dp, mp):
        self.dp, self.mp = dp, mp
        mp_bits = [("mp", 1 << k) for k in range(mp.bit_length() - 1)]
        z_bits = [("dp", 2 << k) for k in range(dp.bit_length() - 2)]
        low, high = mp_bits[0], mp_bits[len(mp_bits) // 2]
        self.other = [bit for bit in mp_bits if bit not in (low, high)]
        self.scatter = [(low, high), (high, low)]
        rest = self.other + z_bits
        self.rest = list(zip(rest, rest[::-1]))
        self.replicas = list(zip(z_bits, z_bits[::-1]))
        self.low, self.high = low, high

    def send(self, x, step):
        pairs = []
        for d in range(self.dp):
            for m in range(self.mp):
                axis, bit = step[d % 2]
                to = (d ^ bit) * self.mp + m if axis == "dp" else d * self.mp + (m ^ bit)
                pairs.append((d * self.mp + m, to))
        return lax.ppermute(x, AXES, pairs)

    def core(self, x):
        return self.send(x, (("dp", 1), ("dp", 1)))


def on_device(dp, mp, grad, error, init):
    grad, error = grad[0], error[0]
    rows, cols = grad.shape
    rank = init.shape[1]
    half = rank // 2
    net = Exchange(dp, mp)
    place = [lax.axis_index(axis).astype(jnp.int32).reshape(1) for axis in AXES]
    units = cols // 8 // LANES
    square = (rank, LANES)

    comp, near, far = left_product(net, place, grad, error, init)
    near = near + net.core(far)
    for step in net.replicas:
        sent = lax.reduce_precision(near, 8, 7)
        near = sent + net.send(sent.astype(BF16), step).astype(F32)
    near = near.astype(BF16)
    far = net.core(near)

    def right(side, places, dtype):
        return right_product(net, place, side, places, units, comp, near, far, dtype)

    across = net.core(right(FAR, (2, 3), BF16))
    part = right(NEAR, (2, 3), F32)
    sent, gram = call(
        first_kernel, "first_sum",
        [shaped((2 * units + 2, *square), BF16), shaped((rank, rank), F32)],
        [VMEM] * 4, 4, 0.5, out_specs=[VMEM] * 2,
    )(part, across, near, far)
    arrived = net.send(sent, net.scatter[0])
    across = net.core(right(FAR, (0, 1), BF16))
    part = right(NEAR, (0, 1), F32)
    sent, kept, gram = call(
        second_kernel, "second_sum",
        [shaped((units + 2, *square), BF16), shaped((units, *square), F32), shaped((rank, rank), F32)],
        [VMEM] * 4, 4, 0.5, out_specs=[VMEM] * 3,
    )(part, across, arrived, gram)
    arrived = net.send(sent, net.scatter[1])
    sent, kept, gram = call(
        functools.partial(third_kernel, net), "third_sum",
        [shaped((units, half, LANES), BF16), shaped((units, half, LANES), F32), shaped((rank, rank), F32)],
        [SMEM] * 2 + [VMEM] * 3, 4, 0.5, out_specs=[VMEM] * 3,
        scratch_shapes=[pltpu.VMEM(square, F32)],
    )(*place, kept, arrived, gram)
    for bit in net.other:
        gram = gram + net.send(gram, (bit, bit))

    leaves = list(range(rank // LEAF))
    steps = len(net.rest) + 1
    state = gram
    for k in range(steps):
        share = leaves[len(leaves) * k // steps : len(leaves) * (k + 1) // steps]
        arrived = net.send(sent, net.rest[k] if k < len(net.rest) else net.rest[0])
        state = inverse_part(state, share)
        arrived, state = lax.optimization_barrier((arrived, state))
        if k < len(net.rest):
            sent = call(
                add_kernel, "pair_sum", shaped((units, half, LANES), BF16), [VMEM] * 2, 2, 0.3, out_specs=VMEM
            )(kept, arrived)
            kept = sent
    own = call(
        functools.partial(factor_kernel, net), "factor", shaped((units, *square), BF16),
        [SMEM] * 2 + [VMEM] * 3, 4, 0.7, out_specs=VMEM,
        scratch_shapes=[pltpu.VMEM((rank, units * LANES), BF16)],
    )(*place, sent, arrived, state)

    arrived = net.send(own, net.scatter[1])
    base_near, base_far = call(
        base_kernel, "base", [shaped((rows // 2, rank), BF16)] * 2, [VMEM] * 3, 4, 0.7, out_specs=[VMEM] * 2
    )(near, far, state)
    arrived, base_near, base_far = lax.optimization_barrier((arrived, base_near, base_far))
    write = functools.partial(new_error, net, place, units=units, comp=comp, near=base_near, far=base_far)
    own = jnp.concatenate([own, arrived], axis=0)
    arrived = net.send(own, net.scatter[0])
    other = net.core(own)
    out = write(NEAR, (0, 1), own)
    out = write(FAR, (0, 1), other, held=out)
    share, width = cols // mp, units * LANES
    if share == 2 * width:
        right_factor = call(
            functools.partial(rows_kernel, net, units), "factor_rows", shaped((share, rank), BF16),
            [SMEM, SMEM, VMEM, VMEM], 4, 1, out_specs=VMEM,
        )(*place, own, other)
        arrived, out, right_factor = lax.optimization_barrier((arrived, out, right_factor))
    else:
        arrived, out = lax.optimization_barrier((arrived, out))
    crossed = net.core(arrived)
    out = write(NEAR, (2, 3), arrived, held=out)
    out = write(FAR, (2, 3), crossed, held=out)
    if share != 2 * width:
        everything = jnp.concatenate([own, arrived, other, crossed], axis=0)
        here = Place(net, place)
        names = jnp.stack([here.block(side, k) for side in (NEAR, FAR) for k in range(4)])
        block = here.mp * share // width
        chosen = lax.dynamic_slice_in_dim(everything, jnp.argmax(names == block) * units, units, 0)
        chosen = jnp.swapaxes(chosen, 1, 2).reshape(width, rank)
        right_factor = lax.dynamic_slice_in_dim(chosen, here.mp * share - block * width, share, 0)
    return (out[None], right_factor)


def solution(mesh):
    return jax.shard_map(
        functools.partial(on_device, mesh.shape["dp"], mesh.shape["mp"]),
        mesh=mesh,
        in_specs=(P("dp", "mp", None), P("dp", "mp", None), P()),
        out_specs=(P("dp", "mp", None), P("mp", None)),
        check_vma=False,
    )
```

```python
import functools

import jax
import jax.numpy as jnp
from jax import lax
from jax.experimental import pallas as pl
from jax.experimental.pallas import tpu as pltpu
from jax.sharding import PartitionSpec as P

F32 = jnp.float32
BF16 = jnp.bfloat16
LANES = 128
MIB = 1024 * 1024
AXES = ("dp", "mp")
PIECES = 14
LEAF = 8

VMEM = pl.BlockSpec(memory_space=pltpu.VMEM)
HBM = pl.BlockSpec(memory_space=pltpu.HBM)
SMEM = pl.BlockSpec(memory_space=pltpu.SMEM)

NEAR, FAR = 0, 1


class Place:
    def __init__(self, net, place):
        self.net = net
        self.dp, self.mp = place[0][0], place[1][0]
        self.core = self.dp & 1

    def half(self, side):
        return self.core if side == NEAR else 1 - self.core

    def bit(self, name):
        axis, value = name
        return ((self.dp if axis == "dp" else self.mp) >> (value.bit_length() - 1)) & 1

    def block(self, side, k):
        core = self.half(side)
        a, b = k // 2, k % 2
        low = self.bit(self.net.low) ^ (a + (b - a) * core)
        high = self.bit(self.net.high) ^ (b + (a - b) * core)
        return high * 4 + low * 2 + core


def call(kernel, name, outs, ins, vmem_mib, micros, **more):
    return pl.pallas_call(
        kernel,
        out_shape=outs,
        in_specs=ins,
        compiler_params=pltpu.CompilerParams(vmem_limit_bytes=vmem_mib * MIB),
        cost_estimate=pl.CostEstimate(flops=0, bytes_accessed=int(micros * 3.5e6), transcendentals=0),
        name=name,
        **more,
    )


def shaped(shape, dtype):
    return jax.ShapeDtypeStruct(shape, dtype)


def in_hbm(x):
    return pltpu.with_memory_space_constraint(x, pltpu.HBM)


def in_vmem(x):
    return pltpu.with_memory_space_constraint(x, pltpu.VMEM)


def left_kernel(net, pieces, dp, mp, grad, error, init, comp, near, far, error_v, init_v, sems):
    place = Place(net, (dp, mp))
    rows, cols = comp.shape
    count, width = rows // 2, cols // pieces

    def copies(i):
        at = pl.ds(i * width, width)
        out = [pltpu.make_async_copy(init.at[at], init_v.at[at], sems.at[4, i])]
        for half in range(2):
            source = pl.ds(pl.multiple_of(place.half(half) * count, count), count)
            target = pl.ds(half * count, count)
            out.append(pltpu.make_async_copy(grad.at[source, at], comp.at[target, at], sems.at[half, i]))
            out.append(pltpu.make_async_copy(error.at[source, at], error_v.at[target, at], sems.at[2 + half, i]))
        return out

    for i in range(pieces):
        for copy in copies(i):
            copy.start()
    for i in range(pieces):
        for copy in copies(i):
            copy.wait()
        at = pl.ds(i * width, width)
        total = (comp[:, at].astype(F32) + error_v[:, at].astype(F32)).astype(BF16)
        comp[:, at] = total
        part = lax.dot_general(init_v[at].T, total, (((1,), (1,)), ((), ())), preferred_element_type=F32)
        if i == 0:
            near[...] = part[:, :count]
            far[...] = part[:, count:]
        else:
            near[...] += part[:, :count]
            far[...] += part[:, count:]


def left_product(net, place, grad, error, init):
    rows, cols = grad.shape
    rank = init.shape[1]
    return call(
        functools.partial(left_kernel, net, PIECES),
        "left_product",
        [pltpu.VMEM((rows, cols), BF16), shaped((rank, rows // 2), F32), shaped((rank, rows // 2), F32)],
        [SMEM, SMEM, HBM, HBM, HBM],
        26,
        12,
        out_specs=[VMEM] * 3,
        scratch_shapes=[
            pltpu.VMEM((rows, cols), BF16),
            pltpu.VMEM((cols, rank), BF16),
            pltpu.SemaphoreType.DMA((5, PIECES)),
        ],
    )(*place, in_hbm(grad), in_hbm(error), in_hbm(init))


def right_kernel(net, units, side, places, dp, mp, comp, near, far, out):
    place = Place(net, (dp, mp))
    rows = comp.shape[0]
    count = rows // 2
    for block, k in enumerate(places):
        start = place.block(side, k) * (units * LANES)
        for unit in range(0, units, 2):
            wide = min(2, units - unit)
            at = pl.ds(pl.multiple_of(start + unit * LANES, LANES), wide * LANES)
            product = jnp.dot(near[...], comp[:count, at], preferred_element_type=F32)
            product += jnp.dot(far[...], comp[count:, at], preferred_element_type=F32)
            for k in range(wide):
                out[block * units + unit + k] = product[:, k * LANES : (k + 1) * LANES].astype(out.dtype)


def right_product(net, place, side, places, units, comp, near, far, dtype):
    rank = near.shape[0]
    return call(
        functools.partial(right_kernel, net, units, side, places),
        "right_product",
        shaped((len(places) * units, rank, LANES), dtype),
        [SMEM, SMEM, VMEM, VMEM, VMEM],
        4,
        0.7 * len(places),
        out_specs=VMEM,
    )(*place, in_vmem(comp), near, far)


def new_error_kernel(net, units, side, places, dp, mp, comp, near, far, right, *rest):
    place = Place(net, (dp, mp))
    out, buf, sems = rest[-3:]
    count = comp.shape[0] // 2
    width = units * LANES
    copies = []
    for j, k in enumerate(places):
        start = pl.multiple_of(place.block(side, k) * width, LANES)
        for half, base in enumerate((near, far)):
            for unit in range(0, units, 2):
                wide = min(2, units - unit)
                factor = [right[j * units + unit + i] for i in range(wide)]
                factor = jnp.concatenate(factor, axis=1) if wide > 1 else factor[0]
                product = jnp.dot(base[...], factor, preferred_element_type=F32)
                at = pl.ds(pl.multiple_of(start + unit * LANES, LANES), wide * LANES)
                kept = comp[half * count : (half + 1) * count, at].astype(F32)
                here = pl.ds(unit * LANES, wide * LANES)
                buf[half, j, :, here] = (kept - product).astype(BF16)
                rows = pl.ds(pl.multiple_of(place.half(half) * count, count), count)
                copy = pltpu.make_async_copy(
                    buf.at[half, j, :, here], out.at[rows, at], sems.at[half, j, unit // 2]
                )
                copy.start()
                copies.append(copy)
    for copy in copies:
        copy.wait()


def new_error(net, place, side, places, right, units, comp, near, far, held=None):
    rows, cols = comp.shape
    extra = [] if held is None else [in_hbm(held)]
    return call(
        functools.partial(new_error_kernel, net, units, side, places),
        "new_error",
        shaped((rows, cols), BF16),
        [SMEM] * 2 + [VMEM] * 4 + [HBM] * len(extra),
        12,
        1 + 0.7 * len(places),
        out_specs=HBM,
        scratch_shapes=[
            pltpu.VMEM((2, len(places), rows // 2, units * LANES), BF16),
            pltpu.SemaphoreType.DMA((2, len(places), (units + 1) // 2)),
        ],
        input_output_aliases={6: 0} if extra else {},
    )(*place, in_vmem(comp), near, far, right, *extra)


def leaf_steps(state, leaf):
    n, b = state.shape[0], LEAF
    base = leaf * b

    def splat(v):
        return jnp.broadcast_to(v, (b, n))

    def column(tile, j):
        return splat(state[b * tile : b * tile + b, base + j : base + j + 1])

    here = [column(leaf, j) for j in range(b)]
    a = [[splat(here[j][i : i + 1]) if j <= i else None for j in range(b)] for i in range(b)]
    mult = [[None] * b for _ in range(b)]
    unit = [[None] * b for _ in range(b)]
    recip, scale = [], []
    for k in range(b):
        recip.append(1.0 / a[k][k])
        scale.append(lax.rsqrt(a[k][k]))
        for i in range(k + 1, b):
            mult[i][k] = a[i][k] * recip[k]
        for i in range(k + 1, b):
            for j in range(k + 1, i + 1):
                a[i][j] = a[i][j] - mult[i][k] * a[j][k]
    for j in range(b):
        for i in range(j + 1, b):
            total = mult[i][j]
            for k in range(j + 1, i):
                total = total + mult[i][k] * unit[k][j]
            unit[i][j] = -total
    rows_x = [splat(state[base + j : base + j + 1, n:]) for j in range(b)]
    if leaf + 1 < n // b:
        rows_g = [splat(state[base + j : base + j + 1, :n]) for j in range(b)]

        def term(k, j):
            return recip[k] if j == k else recip[k] * unit[k][j]

        inverse = [[None] * b for _ in range(b)]
        for i in range(b):
            for j in range(i + 1):
                total = term(i, j)
                for k in range(i + 1, b):
                    total = total + unit[k][i] * term(k, j)
                inverse[i][j] = inverse[j][i] = total

        def mixed(rows):
            out = []
            for k in range(b):
                total = inverse[k][0] * rows[0]
                for j in range(1, b):
                    total = total + inverse[k][j] * rows[j]
                out.append(total)
            return out

        mixed_g, mixed_x = mixed(rows_g), mixed(rows_x)
        for tile in range(leaf + 1, n // b):
            at = slice(b * tile, b * tile + b)
            columns = [column(tile, j) for j in range(b)]
            g, x = state[at, :n], state[at, n:]
            for k in range(b):
                g = g - columns[k] * mixed_g[k]
                x = x - columns[k] * mixed_x[k]
            state[at, :n] = g
            state[at, n:] = x
    for i in range(b):
        total = rows_x[i]
        for j in range(i):
            total = total + unit[i][j] * rows_x[j]
        state[base + i : base + i + 1, n:] = (total * scale[i])[:1]


def leaves_kernel(leaves, source, state):
    n = state.shape[0]
    if source.shape == state.shape:
        state[...] = source[...]
    else:
        state[:, :n] = source[...]
        row = lax.broadcasted_iota(jnp.int32, (n, n), 0)
        state[:, n:] = (row == lax.broadcasted_iota(jnp.int32, (n, n), 1)).astype(F32)
    for leaf in leaves:
        leaf_steps(state, leaf)


def inverse_part(source, leaves):
    n = source.shape[0]
    return call(
        functools.partial(leaves_kernel, leaves),
        "inverse_part",
        shaped((n, 2 * n), F32),
        [VMEM],
        4,
        1.5,
        out_specs=VMEM,
    )(source)


def split2(x):
    high = x.astype(BF16)
    return high, (x - high.astype(F32)).astype(BF16)


def put2(ref, at, x):
    ref[at], ref[at + 1] = split2(x)


def get2(ref, at):
    return ref[at].astype(F32) + ref[at + 1].astype(F32)


def first_kernel(part, arrived, near, far, out, gram):
    count = part.shape[0]
    contract = (((1,), (1,)), ((), ()))
    total = lax.dot_general(near[...], near[...], contract, preferred_element_type=F32)
    total += lax.dot_general(far[...], far[...], contract, preferred_element_type=F32)
    gram[...] = total
    put2(out, count, total)

    for i in range(count):
        out[i] = (part[i] + arrived[i].astype(F32)).astype(BF16)


def second_kernel(part, across, arrived, gram_in, out, kept, gram):
    units = kept.shape[0]
    total = gram_in[...] + get2(arrived, 2 * units)
    gram[...] = total
    put2(out, units, total)

    for i in range(units):
        j = i + units
        out[i] = (part[j] + across[j].astype(F32) + arrived[j].astype(F32)).astype(BF16)
        kept[i] = part[i] + across[i].astype(F32) + arrived[i].astype(F32)


def third_kernel(part, arrived, gram_in, out, gram):
    units = part.shape[0]
    gram[...] = gram_in[...] + get2(arrived, units)
    for i in range(units):
        out[i] = (part[i] + arrived[i].astype(F32)).astype(BF16)


def add_kernel(kept, arrived, out):
    for i in range(kept.shape[0]):
        out[i] = (kept[i].astype(F32) + arrived[i].astype(F32)).astype(BF16)


def factor_kernel(replicas, own, arrived, state, out):
    units, rank = own.shape[:2]
    lhs = jnp.concatenate(split2(state[:, rank:]), axis=0)
    for i in range(0, units, 2):
        some = range(i, min(i + 2, units))
        summed = [(own[k].astype(F32) + arrived[k].astype(F32)).astype(BF16) for k in some]
        summed = jnp.concatenate(summed, axis=1) if len(summed) > 1 else summed[0]
        product = jnp.dot(lhs, summed, preferred_element_type=F32)
        product = (product[:rank] + product[rank:]) / replicas
        for k in some:
            out[k] = product[:, (k - i) * LANES : (k - i + 1) * LANES].astype(BF16)


def base_kernel(near, far, state, near_out, far_out):
    rank = near.shape[0]
    lhs = jnp.concatenate(split2(state[:, rank:]), axis=0)
    for source, out in ((near, near_out), (far, far_out)):
        product = jnp.dot(lhs, source[...], preferred_element_type=F32)
        out[...] = (product[:rank] + product[rank:]).T.astype(BF16)


def rows_kernel(net, units, dp, mp, own, other, out):
    place = Place(net, (dp, mp))
    for side, source in ((NEAR, own), (FAR, other)):
        start = place.half(side) * (units * LANES)
        for i in range(units):
            out[pl.ds(pl.multiple_of(start + i * LANES, LANES), LANES), :] = source[i].T


class Exchange:
    def __init__(self, dp, mp):
        self.dp, self.mp = dp, mp
        mp_bits = [("mp", 1 << k) for k in range(mp.bit_length() - 1)]
        z_bits = [("dp", 2 << k) for k in range(dp.bit_length() - 2)]
        low, high = mp_bits[0], mp_bits[len(mp_bits) // 2]
        self.other = [bit for bit in mp_bits if bit not in (low, high)]
        self.scatter = [(low, high), (high, low)]
        rest = self.other + z_bits
        self.rest = list(zip(rest, rest[::-1]))
        self.replicas = list(zip(z_bits, z_bits[::-1]))
        self.low, self.high = low, high

    def send(self, x, step):
        pairs = []
        for d in range(self.dp):
            for m in range(self.mp):
                axis, bit = step[d % 2]
                to = (d ^ bit) * self.mp + m if axis == "dp" else d * self.mp + (m ^ bit)
                pairs.append((d * self.mp + m, to))
        return lax.ppermute(x, AXES, pairs)

    def core(self, x):
        return self.send(x, (("dp", 1), ("dp", 1)))


def on_device(dp, mp, grad, error, init):
    grad, error = grad[0], error[0]
    rows, cols = grad.shape
    rank = init.shape[1]
    net = Exchange(dp, mp)
    place = [lax.axis_index(axis).astype(jnp.int32).reshape(1) for axis in AXES]
    units = cols // 8 // LANES
    square = (rank, LANES)

    comp, near, far = left_product(net, place, grad, error, init)
    near = near + net.core(far)
    for step in net.replicas:
        sent = lax.reduce_precision(near, 8, 7)
        near = sent + net.send(sent.astype(BF16), step).astype(F32)
    near = near.astype(BF16)
    far = net.core(near)

    def right(side, places, dtype):
        return right_product(net, place, side, places, units, comp, near, far, dtype)

    across = net.core(right(FAR, (2, 3), BF16))
    part = right(NEAR, (2, 3), F32)
    sent, gram = call(
        first_kernel, "first_sum",
        [shaped((2 * units + 2, *square), BF16), shaped((rank, rank), F32)],
        [VMEM] * 4, 4, 0.5, out_specs=[VMEM] * 2,
    )(part, across, near, far)
    arrived = net.send(sent, net.scatter[0])
    across = net.core(right(FAR, (0, 1), BF16))
    part = right(NEAR, (0, 1), F32)
    sent, kept, gram = call(
        second_kernel, "second_sum",
        [shaped((units + 2, *square), BF16), shaped((units, *square), F32), shaped((rank, rank), F32)],
        [VMEM] * 4, 4, 0.5, out_specs=[VMEM] * 3,
    )(part, across, arrived, gram)
    arrived = net.send(sent, net.scatter[1])
    sent, gram = call(
        third_kernel, "third_sum",
        [shaped((units, *square), BF16), shaped((rank, rank), F32)],
        [VMEM] * 3, 4, 0.5, out_specs=[VMEM] * 2,
    )(kept, arrived, gram)
    for bit in net.other:
        gram = gram + net.send(gram, (bit, bit))

    leaves = list(range(rank // LEAF))
    steps = len(net.rest)
    state = gram
    for k, step in enumerate(net.rest):
        arrived = net.send(sent, step)
        state = inverse_part(state, leaves[len(leaves) * k // steps : len(leaves) * (k + 1) // steps])
        arrived, state = lax.optimization_barrier((arrived, state))
        if k < steps - 1:
            sent = call(
                add_kernel, "pair_sum", shaped((units, *square), BF16), [VMEM] * 2, 2, 0.3, out_specs=VMEM
            )(sent, arrived)
    own = call(
        functools.partial(factor_kernel, dp), "factor", shaped((units, *square), BF16),
        [VMEM] * 3, 4, 0.7, out_specs=VMEM,
    )(sent, arrived, state)

    arrived = net.send(own, net.scatter[1])
    base_near, base_far = call(
        base_kernel, "base", [shaped((rows // 2, rank), BF16)] * 2, [VMEM] * 3, 4, 0.7, out_specs=[VMEM] * 2
    )(near, far, state)
    arrived, base_near, base_far = lax.optimization_barrier((arrived, base_near, base_far))
    write = functools.partial(new_error, net, place, units=units, comp=comp, near=base_near, far=base_far)
    own = jnp.concatenate([own, arrived], axis=0)
    arrived = net.send(own, net.scatter[0])
    other = net.core(own)
    out = write(NEAR, (0, 1), own)
    out = write(FAR, (0, 1), other, held=out)
    share, width = cols // mp, units * LANES
    if share == 2 * width:
        right_factor = call(
            functools.partial(rows_kernel, net, units), "factor_rows", shaped((share, rank), BF16),
            [SMEM, SMEM, VMEM, VMEM], 4, 1, out_specs=VMEM,
        )(*place, own, other)
        arrived, out, right_factor = lax.optimization_barrier((arrived, out, right_factor))
    else:
        arrived, out = lax.optimization_barrier((arrived, out))
    crossed = net.core(arrived)
    out = write(NEAR, (2, 3), arrived, held=out)
    out = write(FAR, (2, 3), crossed, held=out)
    if share != 2 * width:
        everything = jnp.concatenate([own, arrived, other, crossed], axis=0)
        here = Place(net, place)
        names = jnp.stack([here.block(side, k) for side in (NEAR, FAR) for k in range(4)])
        block = here.mp * share // width
        chosen = lax.dynamic_slice_in_dim(everything, jnp.argmax(names == block) * units, units, 0)
        chosen = jnp.swapaxes(chosen, 1, 2).reshape(width, rank)
        right_factor = lax.dynamic_slice_in_dim(chosen, here.mp * share - block * width, share, 0)
    return (out[None], right_factor)


def solution(mesh):
    return jax.shard_map(
        functools.partial(on_device, mesh.shape["dp"], mesh.shape["mp"]),
        mesh=mesh,
        in_specs=(P("dp", "mp", None), P("dp", "mp", None), P()),
        out_specs=(P("dp", "mp", None), P("mp", None)),
        check_vma=False,
    )
```

```python
import functools

import jax
import jax.numpy as jnp
from jax import lax
from jax.experimental import pallas as pl
from jax.experimental.pallas import tpu as pltpu
from jax.sharding import PartitionSpec as P

F32 = jnp.float32
BF16 = jnp.bfloat16
LANES = 128
MIB = 1024 * 1024
AXES = ("dp", "mp")
PIECES = 14
LEAF = 8

VMEM = pl.BlockSpec(memory_space=pltpu.VMEM)
HBM = pl.BlockSpec(memory_space=pltpu.HBM)
SMEM = pl.BlockSpec(memory_space=pltpu.SMEM)

NEAR, FAR = 0, 1


class Place:
    def __init__(self, net, place):
        self.net = net
        self.dp, self.mp = place[0][0], place[1][0]
        self.core = self.dp & 1

    def half(self, side):
        return self.core if side == NEAR else 1 - self.core

    def bit(self, name):
        axis, value = name
        return ((self.dp if axis == "dp" else self.mp) >> (value.bit_length() - 1)) & 1

    def block(self, side, k):
        core = self.half(side)
        a, b = k // 2, k % 2
        low = self.bit(self.net.low) ^ (a + (b - a) * core)
        high = self.bit(self.net.high) ^ (b + (a - b) * core)
        return high * 4 + low * 2 + core


def call(kernel, name, outs, ins, vmem_mib, micros, **more):
    return pl.pallas_call(
        kernel,
        out_shape=outs,
        in_specs=ins,
        compiler_params=pltpu.CompilerParams(vmem_limit_bytes=vmem_mib * MIB),
        cost_estimate=pl.CostEstimate(flops=0, bytes_accessed=int(micros * 3.5e6), transcendentals=0),
        name=name,
        **more,
    )


def shaped(shape, dtype):
    return jax.ShapeDtypeStruct(shape, dtype)


def in_hbm(x):
    return pltpu.with_memory_space_constraint(x, pltpu.HBM)


def in_vmem(x):
    return pltpu.with_memory_space_constraint(x, pltpu.VMEM)


def left_kernel(net, pieces, dp, mp, grad, error, init, comp, near, far, error_v, init_v, sems):
    place = Place(net, (dp, mp))
    rows, cols = comp.shape
    count, width = rows // 2, cols // pieces

    def copies(i):
        at = pl.ds(i * width, width)
        out = [pltpu.make_async_copy(init.at[at], init_v.at[at], sems.at[4, i])]
        for half in range(2):
            source = pl.ds(pl.multiple_of(place.half(half) * count, count), count)
            target = pl.ds(half * count, count)
            out.append(pltpu.make_async_copy(grad.at[source, at], comp.at[target, at], sems.at[half, i]))
            out.append(pltpu.make_async_copy(error.at[source, at], error_v.at[target, at], sems.at[2 + half, i]))
        return out

    for i in range(pieces):
        for copy in copies(i):
            copy.start()
    for i in range(pieces):
        for copy in copies(i):
            copy.wait()
        at = pl.ds(i * width, width)
        total = (comp[:, at].astype(F32) + error_v[:, at].astype(F32)).astype(BF16)
        comp[:, at] = total
        part = lax.dot_general(init_v[at].T, total, (((1,), (1,)), ((), ())), preferred_element_type=F32)
        if i == 0:
            near[...] = part[:, :count]
            far[...] = part[:, count:]
        else:
            near[...] += part[:, :count]
            far[...] += part[:, count:]


def left_product(net, place, grad, error, init):
    rows, cols = grad.shape
    rank = init.shape[1]
    return call(
        functools.partial(left_kernel, net, PIECES),
        "left_product",
        [pltpu.VMEM((rows, cols), BF16), shaped((rank, rows // 2), F32), shaped((rank, rows // 2), F32)],
        [SMEM, SMEM, HBM, HBM, HBM],
        26,
        12,
        out_specs=[VMEM] * 3,
        scratch_shapes=[
            pltpu.VMEM((rows, cols), BF16),
            pltpu.VMEM((cols, rank), BF16),
            pltpu.SemaphoreType.DMA((5, PIECES)),
        ],
    )(*place, in_hbm(grad), in_hbm(error), in_hbm(init))


def right_kernel(net, units, side, places, dp, mp, comp, near, far, out):
    place = Place(net, (dp, mp))
    rows = comp.shape[0]
    count = rows // 2
    for block, k in enumerate(places):
        start = place.block(side, k) * (units * LANES)
        for unit in range(0, units, 2):
            wide = min(2, units - unit)
            at = pl.ds(pl.multiple_of(start + unit * LANES, LANES), wide * LANES)
            product = jnp.dot(near[...], comp[:count, at], preferred_element_type=F32)
            product += jnp.dot(far[...], comp[count:, at], preferred_element_type=F32)
            for k in range(wide):
                out[block * units + unit + k] = product[:, k * LANES : (k + 1) * LANES].astype(out.dtype)


def right_product(net, place, side, places, units, comp, near, far, dtype):
    rank = near.shape[0]
    return call(
        functools.partial(right_kernel, net, units, side, places),
        "right_product",
        shaped((len(places) * units, rank, LANES), dtype),
        [SMEM, SMEM, VMEM, VMEM, VMEM],
        4,
        0.7 * len(places),
        out_specs=VMEM,
    )(*place, in_vmem(comp), near, far)


def new_error_kernel(net, units, blocks, dp, mp, comp, near, far, *rest):
    place = Place(net, (dp, mp))
    rights, (out, buf, sems) = rest[: len(blocks)], rest[-3:]
    count = comp.shape[0] // 2
    copies = []
    for j, ((side, k), right) in enumerate(zip(blocks, rights)):
        start = place.block(side, k) * (units * LANES)
        for half, base in enumerate((near, far)):
            rows = pl.ds(pl.multiple_of(place.half(half) * count, count), count)
            for unit in range(0, units, 2):
                wide = min(2, units - unit)
                factor = [right[unit + i] for i in range(wide)]
                factor = jnp.concatenate(factor, axis=1) if wide > 1 else factor[0]
                product = jnp.dot(base[...], factor, preferred_element_type=F32)
                at = pl.ds(pl.multiple_of(start + unit * LANES, LANES), wide * LANES)
                kept = comp[half * count : (half + 1) * count, at].astype(F32)
                here = pl.ds(unit * LANES, wide * LANES)
                buf[half, j, :, here] = (kept - product).astype(BF16)
                copy = pltpu.make_async_copy(
                    buf.at[half, j, :, here], out.at[rows, at], sems.at[half, j, unit // 2]
                )
                copy.start()
                copies.append(copy)
    for copy in copies:
        copy.wait()


def new_error(net, place, blocks, rights, units, comp, near, far, held=None):
    rows, cols = comp.shape
    extra = [] if held is None else [in_hbm(held)]
    return call(
        functools.partial(new_error_kernel, net, units, blocks),
        "new_error",
        shaped((rows, cols), BF16),
        [SMEM] * 2 + [VMEM] * (3 + len(blocks)) + [HBM] * len(extra),
        12,
        0.6 + 0.8 * len(blocks),
        out_specs=HBM,
        scratch_shapes=[
            pltpu.VMEM((2, len(blocks), rows // 2, units * LANES), BF16),
            pltpu.SemaphoreType.DMA((2, len(blocks), (units + 1) // 2)),
        ],
        input_output_aliases={5 + len(blocks): 0} if extra else {},
    )(*place, in_vmem(comp), near, far, *rights, *extra)


def leaf_steps(state, leaf):
    n, b = state.shape[0], LEAF
    base = leaf * b

    def splat(v):
        return jnp.broadcast_to(v, (b, n))

    def column(tile, j):
        return splat(state[b * tile : b * tile + b, base + j : base + j + 1])

    here = [column(leaf, j) for j in range(b)]
    a = [[splat(here[j][i : i + 1]) if j <= i else None for j in range(b)] for i in range(b)]
    mult = [[None] * b for _ in range(b)]
    unit = [[None] * b for _ in range(b)]
    recip, scale = [], []
    for k in range(b):
        recip.append(1.0 / a[k][k])
        scale.append(lax.rsqrt(a[k][k]))
        for i in range(k + 1, b):
            mult[i][k] = a[i][k] * recip[k]
        for i in range(k + 1, b):
            for j in range(k + 1, i + 1):
                a[i][j] = a[i][j] - mult[i][k] * a[j][k]
    for j in range(b):
        for i in range(j + 1, b):
            total = mult[i][j]
            for k in range(j + 1, i):
                total = total + mult[i][k] * unit[k][j]
            unit[i][j] = -total
    rows_x = [splat(state[base + j : base + j + 1, n:]) for j in range(b)]
    if leaf + 1 < n // b:
        rows_g = [splat(state[base + j : base + j + 1, :n]) for j in range(b)]

        def term(k, j):
            return recip[k] if j == k else recip[k] * unit[k][j]

        inverse = [[None] * b for _ in range(b)]
        for i in range(b):
            for j in range(i + 1):
                total = term(i, j)
                for k in range(i + 1, b):
                    total = total + unit[k][i] * term(k, j)
                inverse[i][j] = inverse[j][i] = total

        def mixed(rows):
            out = []
            for k in range(b):
                total = inverse[k][0] * rows[0]
                for j in range(1, b):
                    total = total + inverse[k][j] * rows[j]
                out.append(total)
            return out

        mixed_g, mixed_x = mixed(rows_g), mixed(rows_x)
        for tile in range(leaf + 1, n // b):
            at = slice(b * tile, b * tile + b)
            columns = [column(tile, j) for j in range(b)]
            g, x = state[at, :n], state[at, n:]
            for k in range(b):
                g = g - columns[k] * mixed_g[k]
                x = x - columns[k] * mixed_x[k]
            state[at, :n] = g
            state[at, n:] = x
    for i in range(b):
        total = rows_x[i]
        for j in range(i):
            total = total + unit[i][j] * rows_x[j]
        state[base + i : base + i + 1, n:] = (total * scale[i])[:1]


def leaves_kernel(leaves, source, state):
    n = state.shape[0]
    if source.shape == state.shape:
        state[...] = source[...]
    else:
        state[:, :n] = source[...]
        row = lax.broadcasted_iota(jnp.int32, (n, n), 0)
        state[:, n:] = (row == lax.broadcasted_iota(jnp.int32, (n, n), 1)).astype(F32)
    for leaf in leaves:
        leaf_steps(state, leaf)


def inverse_part(source, leaves):
    n = source.shape[0]
    return call(
        functools.partial(leaves_kernel, leaves),
        "inverse_part",
        shaped((n, 2 * n), F32),
        [VMEM],
        4,
        1.5,
        out_specs=VMEM,
    )(source)


def split2(x):
    high = x.astype(BF16)
    return high, (x - high.astype(F32)).astype(BF16)


def first_kernel(part, across, near, far, out, gram):
    units = part.shape[0]
    contract = (((1,), (1,)), ((), ()))
    total = lax.dot_general(near[...], near[...], contract, preferred_element_type=F32)
    total += lax.dot_general(far[...], far[...], contract, preferred_element_type=F32)
    out[units], out[units + 1] = split2(total)
    gram[...] = out[units].astype(F32) + out[units + 1].astype(F32)
    for i in range(units):
        out[i] = (part[i] + across[i].astype(F32)).astype(BF16)


def second_kernel(part, across, arrived, out):
    for i in range(out.shape[0]):
        out[i] = (part[i] + across[i].astype(F32) + arrived[i].astype(F32)).astype(BF16)


def kept_kernel(part, across, arrived, gram_in, out, gram):
    units = out.shape[0]
    gram[...] = gram_in[...] + (arrived[units].astype(F32) + arrived[units + 1].astype(F32))
    for i in range(units):
        out[i] = part[i] + across[i].astype(F32) + arrived[i].astype(F32)


def add_kernel(one, other, out):
    for i in range(one.shape[0]):
        out[i] = (one[i].astype(F32) + other[i].astype(F32)).astype(BF16)


def factor_kernel(replicas, own, arrived, state, out):
    units, rank = own.shape[:2]
    lhs = jnp.concatenate(split2(state[:, rank:]), axis=0)
    for i in range(0, units, 2):
        some = range(i, min(i + 2, units))
        summed = [(own[k].astype(F32) + arrived[k].astype(F32)).astype(BF16) for k in some]
        summed = jnp.concatenate(summed, axis=1) if len(summed) > 1 else summed[0]
        product = jnp.dot(lhs, summed, preferred_element_type=F32)
        product = (product[:rank] + product[rank:]) / replicas
        for k in some:
            out[k] = product[:, (k - i) * LANES : (k - i + 1) * LANES].astype(BF16)


def base_kernel(near, far, state, near_out, far_out):
    rank = near.shape[0]
    lhs = jnp.concatenate(split2(state[:, rank:]), axis=0)
    for source, out in ((near, near_out), (far, far_out)):
        product = jnp.dot(lhs, source[...], preferred_element_type=F32)
        out[...] = (product[:rank] + product[rank:]).T.astype(BF16)


def rows_kernel(net, units, dp, mp, own, other, out):
    place = Place(net, (dp, mp))
    for side, source in ((NEAR, own), (FAR, other)):
        start = place.half(side) * (units * LANES)
        for i in range(units):
            out[pl.ds(pl.multiple_of(start + i * LANES, LANES), LANES), :] = source[i].T


class Exchange:
    def __init__(self, dp, mp):
        self.dp, self.mp = dp, mp
        mp_bits = [("mp", 1 << k) for k in range(mp.bit_length() - 1)]
        z_bits = [("dp", 2 << k) for k in range(dp.bit_length() - 2)]
        low, high = mp_bits[0], mp_bits[len(mp_bits) // 2]
        self.other = [bit for bit in mp_bits if bit not in (low, high)]
        self.scatter = [(low, high), (high, low)]
        rest = self.other + z_bits
        self.rest = list(zip(rest, rest[::-1]))
        self.replicas = list(zip(z_bits, z_bits[::-1]))
        self.low, self.high = low, high

    def send(self, x, step):
        pairs = []
        for d in range(self.dp):
            for m in range(self.mp):
                axis, bit = step[d % 2]
                to = (d ^ bit) * self.mp + m if axis == "dp" else d * self.mp + (m ^ bit)
                pairs.append((d * self.mp + m, to))
        return lax.ppermute(x, AXES, pairs)

    def core(self, x):
        return self.send(x, (("dp", 1), ("dp", 1)))


def on_device(dp, mp, grad, error, init):
    grad, error = grad[0], error[0]
    rows, cols = grad.shape
    rank = init.shape[1]
    net = Exchange(dp, mp)
    place = [lax.axis_index(axis).astype(jnp.int32).reshape(1) for axis in AXES]
    units = cols // 8 // LANES
    square = (rank, LANES)

    comp, near, far = left_product(net, place, grad, error, init)
    near = near + net.core(far)
    for step in net.replicas:
        sent = lax.reduce_precision(near, 8, 7)
        near = sent + net.send(sent.astype(BF16), step).astype(F32)
    near = near.astype(BF16)
    far = net.core(near)

    def right(side, places, dtype):
        return right_product(net, place, side, places, units, comp, near, far, dtype)

    def small(kernel, name, outs, *ins):
        return call(kernel, name, outs, [VMEM] * len(ins), 4, 0.3, out_specs=jax.tree.map(lambda _: VMEM, outs))(*ins)

    block, square_f32 = shaped((units, *square), BF16), shaped((rank, rank), F32)
    across_3 = net.core(right(FAR, (3,), BF16))
    across_2 = net.core(right(FAR, (2,), BF16))
    sent = small(add_kernel, "first_sum", block, right(NEAR, (3,), F32), across_3)
    near, far, sent = lax.optimization_barrier((near, far, sent))
    arrived_1 = net.send(sent, net.scatter[0])
    sent, gram = small(
        first_kernel, "first_sum", [shaped((units + 2, *square), BF16), square_f32],
        right(NEAR, (2,), F32), across_2, near, far,
    )
    near, far, sent = lax.optimization_barrier((near, far, sent))
    arrived_0 = net.send(sent, net.scatter[0])
    across = net.core(right(FAR, (1,), BF16))
    part = right(NEAR, (1,), F32)
    near, far, arrived_1 = lax.optimization_barrier((near, far, arrived_1))
    sent = small(second_kernel, "second_sum", block, part, across, arrived_1)
    across = net.core(right(FAR, (0,), BF16))
    part = right(NEAR, (0,), F32)
    arrived = net.send(sent, net.scatter[1])
    kept, gram = small(
        kept_kernel, "second_sum", [shaped((units, *square), F32), square_f32], part, across, arrived_0, gram
    )
    gram = gram + net.send(gram, net.scatter[1])
    for bit in net.other:
        gram = gram + net.send(gram, (bit, bit))
    sent = small(add_kernel, "third_sum", block, kept, arrived)

    leaves = list(range(rank // LEAF))
    steps = len(net.rest)
    state = gram
    for k, step in enumerate(net.rest):
        arrived = net.send(sent, step)
        state = inverse_part(state, leaves[len(leaves) * k // steps : len(leaves) * (k + 1) // steps])
        arrived, state = lax.optimization_barrier((arrived, state))
        if k < steps - 1:
            sent = small(add_kernel, "pair_sum", block, sent, arrived)
    own = small(functools.partial(factor_kernel, dp), "factor", block, sent, arrived, state)

    blocks = [own, net.send(own, net.scatter[1]), net.send(own, net.scatter[0]), None]
    base_near, base_far = small(
        base_kernel, "base", [shaped((rows // 2, rank), BF16)] * 2, near, far, state
    )
    own, base_near, base_far = lax.optimization_barrier((own, base_near, base_far))
    others = [net.core(own)]
    write = functools.partial(new_error, net, place, units=units, comp=comp, near=base_near, far=base_far)
    out = write([(NEAR, 0)], [own])
    share, width = cols // mp, units * LANES
    right_factor = None
    if share == 2 * width:
        right_factor = call(
            functools.partial(rows_kernel, net, units), "factor_rows", shaped((share, rank), BF16),
            [SMEM, SMEM, VMEM, VMEM], 4, 1, out_specs=VMEM,
        )(*place, own, others[0])
    for k in range(1, 4):
        blocks[k], out, right_factor = lax.optimization_barrier((blocks[k], out, right_factor))
        if k == 1:
            blocks[3] = net.send(blocks[1], net.scatter[0])
        others.append(net.core(blocks[k]))
        out = write([(FAR, k - 1), (NEAR, k)], [others[k - 1], blocks[k]], held=out)
    out = write([(FAR, 3)], [others[3]], held=out)
    if right_factor is None:
        everything = jnp.concatenate(blocks + others, axis=0)
        here = Place(net, place)
        names = jnp.stack([here.block(side, k) for side in (NEAR, FAR) for k in range(4)])
        block = here.mp * share // width
        chosen = lax.dynamic_slice_in_dim(everything, jnp.argmax(names == block) * units, units, 0)
        chosen = jnp.swapaxes(chosen, 1, 2).reshape(width, rank)
        right_factor = lax.dynamic_slice_in_dim(chosen, here.mp * share - block * width, share, 0)
    return (out[None], right_factor)


def solution(mesh):
    return jax.shard_map(
        functools.partial(on_device, mesh.shape["dp"], mesh.shape["mp"]),
        mesh=mesh,
        in_specs=(P("dp", "mp", None), P("dp", "mp", None), P()),
        out_specs=(P("dp", "mp", None), P("mp", None)),
        check_vma=False,
    )
```

```python
import functools

import jax
import jax.numpy as jnp
from jax import lax
from jax.experimental import pallas as pl
from jax.experimental.pallas import tpu as pltpu
from jax.sharding import PartitionSpec as P

F32 = jnp.float32
BF16 = jnp.bfloat16
LANES = 128
MIB = 1024 * 1024
AXES = ("dp", "mp")
PIECES = 14
LEAF = 8

VMEM = pl.BlockSpec(memory_space=pltpu.VMEM)
HBM = pl.BlockSpec(memory_space=pltpu.HBM)
SMEM = pl.BlockSpec(memory_space=pltpu.SMEM)

NEAR, FAR = 0, 1


class Place:
    def __init__(self, net, place):
        self.net = net
        self.dp, self.mp = place[0][0], place[1][0]
        self.core = self.dp & 1

    def half(self, side):
        return self.core if side == NEAR else 1 - self.core

    def bit(self, name):
        axis, value = name
        return ((self.dp if axis == "dp" else self.mp) >> (value.bit_length() - 1)) & 1

    def block(self, side, k):
        core = self.half(side)
        a, b = k // 2, k % 2
        low = self.bit(self.net.low) ^ (a + (b - a) * core)
        high = self.bit(self.net.high) ^ (b + (a - b) * core)
        return high * 4 + low * 2 + core


def call(kernel, name, outs, ins, vmem_mib, micros, **more):
    return pl.pallas_call(
        kernel,
        out_shape=outs,
        in_specs=ins,
        compiler_params=pltpu.CompilerParams(vmem_limit_bytes=vmem_mib * MIB),
        cost_estimate=pl.CostEstimate(flops=0, bytes_accessed=int(micros * 3.5e6), transcendentals=0),
        name=name,
        **more,
    )


def shaped(shape, dtype):
    return jax.ShapeDtypeStruct(shape, dtype)


def in_hbm(x):
    return pltpu.with_memory_space_constraint(x, pltpu.HBM)


def in_vmem(x):
    return pltpu.with_memory_space_constraint(x, pltpu.VMEM)


def left_kernel(net, pieces, dp, mp, grad, error, init, comp, near, far, error_v, init_v, sems):
    place = Place(net, (dp, mp))
    rows, cols = comp.shape
    count, width = rows // 2, cols // pieces

    def copies(i):
        at = pl.ds(i * width, width)
        out = [pltpu.make_async_copy(init.at[at], init_v.at[at], sems.at[4, i])]
        for half in range(2):
            source = pl.ds(pl.multiple_of(place.half(half) * count, count), count)
            target = pl.ds(half * count, count)
            out.append(pltpu.make_async_copy(grad.at[source, at], comp.at[target, at], sems.at[half, i]))
            out.append(pltpu.make_async_copy(error.at[source, at], error_v.at[target, at], sems.at[2 + half, i]))
        return out

    for i in range(pieces):
        for copy in copies(i):
            copy.start()
    for i in range(pieces):
        for copy in copies(i):
            copy.wait()
        at = pl.ds(i * width, width)
        total = (comp[:, at].astype(F32) + error_v[:, at].astype(F32)).astype(BF16)
        comp[:, at] = total
        part = lax.dot_general(init_v[at].T, total, (((1,), (1,)), ((), ())), preferred_element_type=F32)
        if i == 0:
            near[...] = part[:, :count]
            far[...] = part[:, count:]
        else:
            near[...] += part[:, :count]
            far[...] += part[:, count:]


def left_product(net, place, grad, error, init):
    rows, cols = grad.shape
    rank = init.shape[1]
    return call(
        functools.partial(left_kernel, net, PIECES),
        "left_product",
        [pltpu.VMEM((rows, cols), BF16), shaped((rank, rows // 2), F32), shaped((rank, rows // 2), F32)],
        [SMEM, SMEM, HBM, HBM, HBM],
        26,
        12,
        out_specs=[VMEM] * 3,
        scratch_shapes=[
            pltpu.VMEM((rows, cols), BF16),
            pltpu.VMEM((cols, rank), BF16),
            pltpu.SemaphoreType.DMA((5, PIECES)),
        ],
    )(*place, in_hbm(grad), in_hbm(error), in_hbm(init))


def right_kernel(net, units, side, places, dp, mp, comp, near, far, out):
    place = Place(net, (dp, mp))
    rows = comp.shape[0]
    count = rows // 2
    for block, k in enumerate(places):
        start = place.block(side, k) * (units * LANES)
        for unit in range(0, units, 2):
            wide = min(2, units - unit)
            at = pl.ds(pl.multiple_of(start + unit * LANES, LANES), wide * LANES)
            product = jnp.dot(near[...], comp[:count, at], preferred_element_type=F32)
            product += jnp.dot(far[...], comp[count:, at], preferred_element_type=F32)
            for k in range(wide):
                out[block * units + unit + k] = product[:, k * LANES : (k + 1) * LANES].astype(out.dtype)


def right_product(net, place, side, places, units, comp, near, far, dtype):
    rank = near.shape[0]
    return call(
        functools.partial(right_kernel, net, units, side, places),
        "right_product",
        shaped((len(places) * units, rank, LANES), dtype),
        [SMEM, SMEM, VMEM, VMEM, VMEM],
        4,
        0.7 * len(places),
        out_specs=VMEM,
    )(*place, in_vmem(comp), near, far)


def new_error_kernel(net, units, blocks, dp, mp, comp, near, far, *rest):
    place = Place(net, (dp, mp))
    rights, (out, buf, sems) = rest[: len(blocks)], rest[-3:]
    count = comp.shape[0] // 2
    copies = []
    for j, ((side, k), right) in enumerate(zip(blocks, rights)):
        start = place.block(side, k) * (units * LANES)
        for half, base in enumerate((near, far)):
            rows = pl.ds(pl.multiple_of(place.half(half) * count, count), count)
            for unit in range(0, units, 2):
                wide = min(2, units - unit)
                factor = [right[unit + i] for i in range(wide)]
                factor = jnp.concatenate(factor, axis=1) if wide > 1 else factor[0]
                product = jnp.dot(base[...], factor, preferred_element_type=F32)
                at = pl.ds(pl.multiple_of(start + unit * LANES, LANES), wide * LANES)
                kept = comp[half * count : (half + 1) * count, at].astype(F32)
                here = pl.ds(unit * LANES, wide * LANES)
                buf[half, j, :, here] = (kept - product).astype(BF16)
                copy = pltpu.make_async_copy(
                    buf.at[half, j, :, here], out.at[rows, at], sems.at[half, j, unit // 2]
                )
                copy.start()
                copies.append(copy)
    for copy in copies:
        copy.wait()


def new_error(net, place, blocks, rights, units, comp, near, far, held=None):
    rows, cols = comp.shape
    extra = [] if held is None else [in_hbm(held)]
    return call(
        functools.partial(new_error_kernel, net, units, blocks),
        "new_error",
        shaped((rows, cols), BF16),
        [SMEM] * 2 + [VMEM] * (3 + len(blocks)) + [HBM] * len(extra),
        12,
        0.6 + 0.8 * len(blocks),
        out_specs=HBM,
        scratch_shapes=[
            pltpu.VMEM((2, len(blocks), rows // 2, units * LANES), BF16),
            pltpu.SemaphoreType.DMA((2, len(blocks), (units + 1) // 2)),
        ],
        input_output_aliases={5 + len(blocks): 0} if extra else {},
    )(*place, in_vmem(comp), near, far, *rights, *extra)


def leaf_steps(state, leaf):
    n, b = state.shape[0], LEAF
    base = leaf * b

    def splat(v):
        return jnp.broadcast_to(v, (b, n))

    def column(tile, j):
        return splat(state[b * tile : b * tile + b, base + j : base + j + 1])

    here = [column(leaf, j) for j in range(b)]
    a = [[splat(here[j][i : i + 1]) if j <= i else None for j in range(b)] for i in range(b)]
    mult = [[None] * b for _ in range(b)]
    unit = [[None] * b for _ in range(b)]
    recip, scale = [], []
    for k in range(b):
        recip.append(1.0 / a[k][k])
        scale.append(lax.rsqrt(a[k][k]))
        for i in range(k + 1, b):
            mult[i][k] = a[i][k] * recip[k]
        for i in range(k + 1, b):
            for j in range(k + 1, i + 1):
                a[i][j] = a[i][j] - mult[i][k] * a[j][k]
    for j in range(b):
        for i in range(j + 1, b):
            total = mult[i][j]
            for k in range(j + 1, i):
                total = total + mult[i][k] * unit[k][j]
            unit[i][j] = -total
    rows_x = [splat(state[base + j : base + j + 1, n:]) for j in range(b)]
    if leaf + 1 < n // b:
        rows_g = [splat(state[base + j : base + j + 1, :n]) for j in range(b)]

        def term(k, j):
            return recip[k] if j == k else recip[k] * unit[k][j]

        inverse = [[None] * b for _ in range(b)]
        for i in range(b):
            for j in range(i + 1):
                total = term(i, j)
                for k in range(i + 1, b):
                    total = total + unit[k][i] * term(k, j)
                inverse[i][j] = inverse[j][i] = total

        def mixed(rows):
            out = []
            for k in range(b):
                total = inverse[k][0] * rows[0]
                for j in range(1, b):
                    total = total + inverse[k][j] * rows[j]
                out.append(total)
            return out

        mixed_g, mixed_x = mixed(rows_g), mixed(rows_x)
        for tile in range(leaf + 1, n // b):
            at = slice(b * tile, b * tile + b)
            columns = [column(tile, j) for j in range(b)]
            g, x = state[at, :n], state[at, n:]
            for k in range(b):
                g = g - columns[k] * mixed_g[k]
                x = x - columns[k] * mixed_x[k]
            state[at, :n] = g
            state[at, n:] = x
    for i in range(b):
        total = rows_x[i]
        for j in range(i):
            total = total + unit[i][j] * rows_x[j]
        state[base + i : base + i + 1, n:] = (total * scale[i])[:1]


def inverse_kernel(gram, state):
    n = state.shape[0]
    state[:, :n] = gram[...]
    row = lax.broadcasted_iota(jnp.int32, (n, n), 0)
    state[:, n:] = (row == lax.broadcasted_iota(jnp.int32, (n, n), 1)).astype(F32)
    for leaf in range(n // LEAF):
        leaf_steps(state, leaf)


def inverse_of(gram):
    n = gram.shape[0]
    return call(inverse_kernel, "inverse", shaped((n, 2 * n), F32), [VMEM], 4, 4.5, out_specs=VMEM)(gram)


def split2(x):
    high = x.astype(BF16)
    return high, (x - high.astype(F32)).astype(BF16)


def first_kernel(part, across, near, far, out, gram):
    units = part.shape[0]
    contract = (((1,), (1,)), ((), ()))
    total = lax.dot_general(near[...], near[...], contract, preferred_element_type=F32)
    total += lax.dot_general(far[...], far[...], contract, preferred_element_type=F32)
    out[units], out[units + 1] = split2(total)
    gram[...] = out[units].astype(F32) + out[units + 1].astype(F32)
    for i in range(units):
        out[i] = (part[i] + across[i].astype(F32)).astype(BF16)


def second_kernel(part, across, arrived, out):
    for i in range(out.shape[0]):
        out[i] = (part[i] + across[i].astype(F32) + arrived[i].astype(F32)).astype(BF16)


def kept_kernel(part, across, arrived, gram_in, out, gram):
    units = out.shape[0]
    gram[...] = gram_in[...] + (arrived[units].astype(F32) + arrived[units + 1].astype(F32))
    for i in range(units):
        out[i] = part[i] + across[i].astype(F32) + arrived[i].astype(F32)


def add_kernel(one, other, out):
    for i in range(one.shape[0]):
        out[i] = (one[i].astype(F32) + other[i].astype(F32)).astype(BF16)


def factor_kernel(replicas, own, arrived, state, out):
    units, rank = own.shape[:2]
    lhs = jnp.concatenate(split2(state[:, rank:]), axis=0)
    for i in range(0, units, 2):
        some = range(i, min(i + 2, units))
        summed = [(own[k].astype(F32) + arrived[k].astype(F32)).astype(BF16) for k in some]
        summed = jnp.concatenate(summed, axis=1) if len(summed) > 1 else summed[0]
        product = jnp.dot(lhs, summed, preferred_element_type=F32)
        product = (product[:rank] + product[rank:]) / replicas
        for k in some:
            out[k] = product[:, (k - i) * LANES : (k - i + 1) * LANES].astype(BF16)


def base_kernel(near, far, state, after, near_out, far_out):
    del after
    rank = near.shape[0]
    lhs = jnp.concatenate(split2(state[:, rank:]), axis=0)
    for source, out in ((near, near_out), (far, far_out)):
        product = jnp.dot(lhs, source[...], preferred_element_type=F32)
        out[...] = (product[:rank] + product[rank:]).T.astype(BF16)


def rows_kernel(net, units, dp, mp, own, other, out):
    place = Place(net, (dp, mp))
    for side, source in ((NEAR, own), (FAR, other)):
        start = place.half(side) * (units * LANES)
        for i in range(units):
            out[pl.ds(pl.multiple_of(start + i * LANES, LANES), LANES), :] = source[i].T


class Exchange:
    def __init__(self, dp, mp):
        self.dp, self.mp = dp, mp
        mp_bits = [("mp", 1 << k) for k in range(mp.bit_length() - 1)]
        z_bits = [("dp", 2 << k) for k in range(dp.bit_length() - 2)]
        low, high = mp_bits[0], mp_bits[len(mp_bits) // 2]
        self.other = [bit for bit in mp_bits if bit not in (low, high)]
        self.scatter = [(low, high), (high, low)]
        rest = self.other + z_bits
        self.rest = list(zip(rest, rest[::-1]))
        self.replicas = list(zip(z_bits, z_bits[::-1]))
        self.low, self.high = low, high

    def send(self, x, step):
        pairs = []
        for d in range(self.dp):
            for m in range(self.mp):
                axis, bit = step[d % 2]
                to = (d ^ bit) * self.mp + m if axis == "dp" else d * self.mp + (m ^ bit)
                pairs.append((d * self.mp + m, to))
        return lax.ppermute(x, AXES, pairs)

    def core(self, x):
        return self.send(x, (("dp", 1), ("dp", 1)))


def on_device(dp, mp, grad, error, init):
    grad, error = grad[0], error[0]
    rows, cols = grad.shape
    rank = init.shape[1]
    net = Exchange(dp, mp)
    place = [lax.axis_index(axis).astype(jnp.int32).reshape(1) for axis in AXES]
    units = cols // 8 // LANES
    square = (rank, LANES)

    comp, near, far = left_product(net, place, grad, error, init)
    near = near + net.core(far)
    for step in net.replicas:
        sent = lax.reduce_precision(near, 8, 7)
        near = sent + net.send(sent.astype(BF16), step).astype(F32)
    near = near.astype(BF16)
    far = net.core(near)

    def right(side, places, dtype):
        return right_product(net, place, side, places, units, comp, near, far, dtype)

    def small(kernel, name, outs, *ins):
        return call(kernel, name, outs, [VMEM] * len(ins), 4, 0.3, out_specs=jax.tree.map(lambda _: VMEM, outs))(*ins)

    block, square_f32 = shaped((units, *square), BF16), shaped((rank, rank), F32)
    across_3 = net.core(right(FAR, (3,), BF16))
    across_2 = net.core(right(FAR, (2,), BF16))
    sent = small(add_kernel, "first_sum", block, right(NEAR, (3,), F32), across_3)
    near, far, sent = lax.optimization_barrier((near, far, sent))
    arrived_1 = net.send(sent, net.scatter[0])
    sent, gram = small(
        first_kernel, "first_sum", [shaped((units + 2, *square), BF16), square_f32],
        right(NEAR, (2,), F32), across_2, near, far,
    )
    near, far, sent = lax.optimization_barrier((near, far, sent))
    arrived_0 = net.send(sent, net.scatter[0])
    across = net.core(right(FAR, (1,), BF16))
    part = right(NEAR, (1,), F32)
    near, far, arrived_1 = lax.optimization_barrier((near, far, arrived_1))
    sent = small(second_kernel, "second_sum", block, part, across, arrived_1)
    across = net.core(right(FAR, (0,), BF16))
    part = right(NEAR, (0,), F32)
    arrived = net.send(sent, net.scatter[1])
    kept, gram = small(
        kept_kernel, "second_sum", [shaped((units, *square), F32), square_f32], part, across, arrived_0, gram
    )
    gram = gram + net.send(gram, net.scatter[1])
    for bit in net.other:
        gram = gram + net.send(gram, (bit, bit))
    sent = small(add_kernel, "third_sum", block, kept, arrived)

    for step in net.rest[:-1]:
        arrived, gram = lax.optimization_barrier((net.send(sent, step), gram))
        sent = small(add_kernel, "pair_sum", block, sent, arrived)
    arrived = net.send(sent, net.rest[-1])
    sent, gram = lax.optimization_barrier((sent, gram))
    arrived, state = lax.optimization_barrier((arrived, inverse_of(gram)))
    own = small(functools.partial(factor_kernel, dp), "factor", block, sent, arrived, state)

    blocks = [own, net.send(own, net.scatter[1]), net.send(own, net.scatter[0]), None]
    base_near, base_far = small(
        base_kernel, "base", [shaped((rows // 2, rank), BF16)] * 2, near, far, state, own
    )
    write = functools.partial(new_error, net, place, units=units, comp=comp, near=base_near, far=base_far)
    out = write([(NEAR, 0)], [own])
    own, out = lax.optimization_barrier((own, out))
    others = [net.core(own)]
    share, width = cols // mp, units * LANES
    right_factor = None
    if share == 2 * width:
        right_factor = call(
            functools.partial(rows_kernel, net, units), "factor_rows", shaped((share, rank), BF16),
            [SMEM, SMEM, VMEM, VMEM], 4, 1, out_specs=VMEM,
        )(*place, own, others[0])
    blocks[1], out = lax.optimization_barrier((blocks[1], out))
    blocks[3] = net.send(blocks[1], net.scatter[0])
    others.append(net.core(blocks[1]))
    blocks[2], out = lax.optimization_barrier((blocks[2], out))
    others.append(net.core(blocks[2]))
    out = write([(FAR, 0), (NEAR, 1), (FAR, 1)], [others[0], blocks[1], others[1]], held=out)
    blocks[3], out, right_factor = lax.optimization_barrier((blocks[3], out, right_factor))
    others.append(net.core(blocks[3]))
    out = write([(NEAR, 2), (FAR, 2)], [blocks[2], others[2]], held=out)
    out = write([(NEAR, 3), (FAR, 3)], [blocks[3], others[3]], held=out)
    if right_factor is None:
        everything = jnp.concatenate(blocks + others, axis=0)
        here = Place(net, place)
        names = jnp.stack([here.block(side, k) for side in (NEAR, FAR) for k in range(4)])
        block = here.mp * share // width
        chosen = lax.dynamic_slice_in_dim(everything, jnp.argmax(names == block) * units, units, 0)
        chosen = jnp.swapaxes(chosen, 1, 2).reshape(width, rank)
        right_factor = lax.dynamic_slice_in_dim(chosen, here.mp * share - block * width, share, 0)
    return (out[None], right_factor)


def solution(mesh):
    return jax.shard_map(
        functools.partial(on_device, mesh.shape["dp"], mesh.shape["mp"]),
        mesh=mesh,
        in_specs=(P("dp", "mp", None), P("dp", "mp", None), P()),
        out_specs=(P("dp", "mp", None), P("mp", None)),
        check_vma=False,
    )
```

```python
import functools

import jax
import jax.numpy as jnp
from jax import lax
from jax.experimental import pallas as pl
from jax.experimental.pallas import tpu as pltpu
from jax.sharding import PartitionSpec as P

F32 = jnp.float32
BF16 = jnp.bfloat16
LANES = 128
MIB = 1024 * 1024
AXES = ("dp", "mp")
PIECES = 14
LEAF = 8

VMEM = pl.BlockSpec(memory_space=pltpu.VMEM)
HBM = pl.BlockSpec(memory_space=pltpu.HBM)
SMEM = pl.BlockSpec(memory_space=pltpu.SMEM)

NEAR, FAR = 0, 1


class Place:
    def __init__(self, net, place):
        self.net = net
        self.dp, self.mp = place[0][0], place[1][0]
        self.core = self.dp & 1

    def half(self, side):
        return self.core if side == NEAR else 1 - self.core

    def bit(self, name):
        axis, value = name
        return ((self.dp if axis == "dp" else self.mp) >> (value.bit_length() - 1)) & 1

    def block(self, side, k):
        core = self.half(side)
        a, b = k // 2, k % 2
        low = self.bit(self.net.low) ^ (a + (b - a) * core)
        high = self.bit(self.net.high) ^ (b + (a - b) * core)
        return high * 4 + low * 2 + core


def call(kernel, name, outs, ins, vmem_mib, micros, **more):
    return pl.pallas_call(
        kernel,
        out_shape=outs,
        in_specs=ins,
        compiler_params=pltpu.CompilerParams(vmem_limit_bytes=vmem_mib * MIB),
        cost_estimate=pl.CostEstimate(flops=0, bytes_accessed=int(micros * 3.5e6), transcendentals=0),
        name=name,
        **more,
    )


def shaped(shape, dtype):
    return jax.ShapeDtypeStruct(shape, dtype)


def in_hbm(x):
    return pltpu.with_memory_space_constraint(x, pltpu.HBM)


def in_vmem(x):
    return pltpu.with_memory_space_constraint(x, pltpu.VMEM)


def left_kernel(net, pieces, dp, mp, grad, error, init, comp, near, far, error_v, init_v, sems):
    place = Place(net, (dp, mp))
    rows, cols = comp.shape
    count, width = rows // 2, cols // pieces

    def copies(i):
        at = pl.ds(i * width, width)
        out = [pltpu.make_async_copy(init.at[at], init_v.at[at], sems.at[4, i])]
        for half in range(2):
            source = pl.ds(pl.multiple_of(place.half(half) * count, count), count)
            target = pl.ds(half * count, count)
            out.append(pltpu.make_async_copy(grad.at[source, at], comp.at[target, at], sems.at[half, i]))
            out.append(pltpu.make_async_copy(error.at[source, at], error_v.at[target, at], sems.at[2 + half, i]))
        return out

    for i in range(pieces):
        for copy in copies(i):
            copy.start()
    for i in range(pieces):
        for copy in copies(i):
            copy.wait()
        at = pl.ds(i * width, width)
        total = (comp[:, at].astype(F32) + error_v[:, at].astype(F32)).astype(BF16)
        comp[:, at] = total
        part = lax.dot_general(init_v[at].T, total, (((1,), (1,)), ((), ())), preferred_element_type=F32)
        if i == 0:
            near[...] = part[:, :count]
            far[...] = part[:, count:]
        else:
            near[...] += part[:, :count]
            far[...] += part[:, count:]


def left_product(net, place, grad, error, init):
    rows, cols = grad.shape
    rank = init.shape[1]
    return call(
        functools.partial(left_kernel, net, PIECES),
        "left_product",
        [pltpu.VMEM((rows, cols), BF16), shaped((rank, rows // 2), F32), shaped((rank, rows // 2), F32)],
        [SMEM, SMEM, HBM, HBM, HBM],
        26,
        12,
        out_specs=[VMEM] * 3,
        scratch_shapes=[
            pltpu.VMEM((rows, cols), BF16),
            pltpu.VMEM((cols, rank), BF16),
            pltpu.SemaphoreType.DMA((5, PIECES)),
        ],
    )(*place, in_hbm(grad), in_hbm(error), in_hbm(init))


def right_kernel(net, units, side, places, dp, mp, comp, near, far, out):
    place = Place(net, (dp, mp))
    rows = comp.shape[0]
    count = rows // 2
    for block, k in enumerate(places):
        start = place.block(side, k) * (units * LANES)
        for unit in range(0, units, 2):
            wide = min(2, units - unit)
            at = pl.ds(pl.multiple_of(start + unit * LANES, LANES), wide * LANES)
            product = jnp.dot(near[...], comp[:count, at], preferred_element_type=F32)
            product += jnp.dot(far[...], comp[count:, at], preferred_element_type=F32)
            for k in range(wide):
                out[block * units + unit + k] = product[:, k * LANES : (k + 1) * LANES].astype(out.dtype)


def right_product(net, place, side, places, units, comp, near, far, dtype):
    rank = near.shape[0]
    return call(
        functools.partial(right_kernel, net, units, side, places),
        "right_product",
        shaped((len(places) * units, rank, LANES), dtype),
        [SMEM, SMEM, VMEM, VMEM, VMEM],
        4,
        0.7 * len(places),
        out_specs=VMEM,
    )(*place, in_vmem(comp), near, far)


def new_error_kernel(net, units, blocks, rows_too, dp, mp, comp, near, far, *rest):
    place = Place(net, (dp, mp))
    rights, rest = rest[: len(blocks)], rest[len(blocks) :]
    count = comp.shape[0] // 2
    copies = []
    if rows_too:
        own, _, out, factor_rows, buf, sems, rows_buf, rows_sem = rest
        for side, source in ((NEAR, own), (FAR, rights[0])):
            start = place.half(side) * (units * LANES)
            for i in range(units):
                rows_buf[pl.ds(pl.multiple_of(start + i * LANES, LANES), LANES), :] = source[i].T
        copies.append(pltpu.make_async_copy(rows_buf, factor_rows, rows_sem))
        copies[0].start()
    else:
        out, buf, sems = rest[-3:]
    step = min(128, count)
    for j, ((side, k), right) in enumerate(zip(blocks, rights)):
        start = place.block(side, k) * (units * LANES)
        for half, base in enumerate((near, far)):
            rows = pl.ds(pl.multiple_of(place.half(half) * count, count), count)
            for unit in range(0, units, 2):
                wide = min(2, units - unit)
                factor = [right[unit + i] for i in range(wide)]
                factor = jnp.concatenate(factor, axis=1) if wide > 1 else factor[0]
                at = pl.ds(pl.multiple_of(start + unit * LANES, LANES), wide * LANES)
                here = pl.ds(unit * LANES, wide * LANES)
                for row in range(0, count, step):
                    product = jnp.dot(base[row : row + step], factor, preferred_element_type=F32)
                    kept = comp[half * count + row : half * count + row + step, at].astype(F32)
                    buf[half, j, row : row + step, here] = (kept - product).astype(BF16)
                copy = pltpu.make_async_copy(
                    buf.at[half, j, :, here], out.at[rows, at], sems.at[half, j, unit // 2]
                )
                copy.start()
                copies.append(copy)
    for copy in copies:
        copy.wait()


def new_error(net, place, blocks, rights, units, comp, near, far, held=None, own=None):
    rows, cols = comp.shape
    rank = near.shape[1]
    extra = [] if own is None else [own]
    outs, scratch = [shaped((rows, cols), BF16)], [
        pltpu.VMEM((2, len(blocks), rows // 2, units * LANES), BF16),
        pltpu.SemaphoreType.DMA((2, len(blocks), (units + 1) // 2)),
    ]
    if own is not None:
        outs.append(shaped((2 * units * LANES, rank), BF16))
        scratch += [pltpu.VMEM((2 * units * LANES, rank), BF16), pltpu.SemaphoreType.DMA]
    held = [] if held is None else [in_hbm(held)]
    out = call(
        functools.partial(new_error_kernel, net, units, blocks, own is not None),
        "new_error",
        outs,
        [SMEM] * 2 + [VMEM] * (3 + len(blocks) + len(extra)) + [HBM] * len(held),
        12,
        0.6 + 0.8 * len(blocks),
        out_specs=[HBM] * len(outs),
        scratch_shapes=scratch,
        input_output_aliases={5 + len(blocks) + len(extra): 0} if held else {},
    )(*place, in_vmem(comp), near, far, *rights, *extra, *held)
    return out[0] if own is None else out


def leaf_steps(state, leaf):
    n, b = state.shape[0], LEAF
    base = leaf * b

    def splat(v):
        return jnp.broadcast_to(v, (b, n))

    def column(tile, j):
        return splat(state[b * tile : b * tile + b, base + j : base + j + 1])

    here = [column(leaf, j) for j in range(b)]
    a = [[splat(here[j][i : i + 1]) if j <= i else None for j in range(b)] for i in range(b)]
    mult = [[None] * b for _ in range(b)]
    unit = [[None] * b for _ in range(b)]
    recip, scale = [], []
    for k in range(b):
        recip.append(1.0 / a[k][k])
        scale.append(lax.rsqrt(a[k][k]))
        for i in range(k + 1, b):
            mult[i][k] = a[i][k] * recip[k]
        for i in range(k + 1, b):
            for j in range(k + 1, i + 1):
                a[i][j] = a[i][j] - mult[i][k] * a[j][k]
    for j in range(b):
        for i in range(j + 1, b):
            total = mult[i][j]
            for k in range(j + 1, i):
                total = total + mult[i][k] * unit[k][j]
            unit[i][j] = -total
    rows_x = [splat(state[base + j : base + j + 1, n:]) for j in range(b)]
    if leaf + 1 < n // b:
        rows_g = [splat(state[base + j : base + j + 1, :n]) for j in range(b)]

        def term(k, j):
            return recip[k] if j == k else recip[k] * unit[k][j]

        inverse = [[None] * b for _ in range(b)]
        for i in range(b):
            for j in range(i + 1):
                total = term(i, j)
                for k in range(i + 1, b):
                    total = total + unit[k][i] * term(k, j)
                inverse[i][j] = inverse[j][i] = total

        def mixed(rows):
            out = []
            for k in range(b):
                total = inverse[k][0] * rows[0]
                for j in range(1, b):
                    total = total + inverse[k][j] * rows[j]
                out.append(total)
            return out

        mixed_g, mixed_x = mixed(rows_g), mixed(rows_x)
        for tile in range(leaf + 1, n // b):
            at = slice(b * tile, b * tile + b)
            columns = [column(tile, j) for j in range(b)]
            g, x = state[at, :n], state[at, n:]
            for k in range(b):
                g = g - columns[k] * mixed_g[k]
                x = x - columns[k] * mixed_x[k]
            state[at, :n] = g
            state[at, n:] = x
    for i in range(b):
        total = rows_x[i]
        for j in range(i):
            total = total + unit[i][j] * rows_x[j]
        state[base + i : base + i + 1, n:] = (total * scale[i])[:1]


def inverse_kernel(gram, state):
    n = state.shape[0]
    state[:, :n] = gram[...]
    row = lax.broadcasted_iota(jnp.int32, (n, n), 0)
    state[:, n:] = (row == lax.broadcasted_iota(jnp.int32, (n, n), 1)).astype(F32)
    for leaf in range(n // LEAF):
        leaf_steps(state, leaf)


def inverse_of(gram):
    n = gram.shape[0]
    return call(inverse_kernel, "inverse", shaped((n, 2 * n), F32), [VMEM], 4, 4.5, out_specs=VMEM)(gram)


def split2(x):
    high = x.astype(BF16)
    return high, (x - high.astype(F32)).astype(BF16)


def first_kernel(part, across, near, far, out, gram):
    units = part.shape[0]
    contract = (((1,), (1,)), ((), ()))
    total = lax.dot_general(near[...], near[...], contract, preferred_element_type=F32)
    total += lax.dot_general(far[...], far[...], contract, preferred_element_type=F32)
    out[units], out[units + 1] = split2(total)
    gram[...] = out[units].astype(F32) + out[units + 1].astype(F32)
    for i in range(units):
        out[i] = (part[i] + across[i].astype(F32)).astype(BF16)


def second_kernel(part, across, arrived, out):
    for i in range(out.shape[0]):
        out[i] = (part[i] + across[i].astype(F32) + arrived[i].astype(F32)).astype(BF16)


def kept_kernel(part, across, arrived, gram_in, out, gram):
    units = out.shape[0]
    gram[...] = gram_in[...] + (arrived[units].astype(F32) + arrived[units + 1].astype(F32))
    for i in range(units):
        out[i] = part[i] + across[i].astype(F32) + arrived[i].astype(F32)


def add_kernel(one, other, out):
    for i in range(one.shape[0]):
        out[i] = (one[i].astype(F32) + other[i].astype(F32)).astype(BF16)


def factor_kernel(replicas, own, arrived, state, out):
    units, rank = own.shape[:2]
    lhs = jnp.concatenate(split2(state[:, rank:]), axis=0)
    for i in range(0, units, 2):
        some = range(i, min(i + 2, units))
        summed = [(own[k].astype(F32) + arrived[k].astype(F32)).astype(BF16) for k in some]
        summed = jnp.concatenate(summed, axis=1) if len(summed) > 1 else summed[0]
        product = jnp.dot(lhs, summed, preferred_element_type=F32)
        product = (product[:rank] + product[rank:]) / replicas
        for k in some:
            out[k] = product[:, (k - i) * LANES : (k - i + 1) * LANES].astype(BF16)


def base_kernel(near, far, state, near_out, far_out):
    rank = near.shape[0]
    lhs = jnp.concatenate(split2(state[:, rank:]), axis=0)
    for source, out in ((near, near_out), (far, far_out)):
        product = jnp.dot(lhs, source[...], preferred_element_type=F32)
        out[...] = (product[:rank] + product[rank:]).T.astype(BF16)


class Exchange:
    def __init__(self, dp, mp):
        self.dp, self.mp = dp, mp
        mp_bits = [("mp", 1 << k) for k in range(mp.bit_length() - 1)]
        z_bits = [("dp", 2 << k) for k in range(dp.bit_length() - 2)]
        low, high = mp_bits[0], mp_bits[len(mp_bits) // 2]
        self.other = [bit for bit in mp_bits if bit not in (low, high)]
        self.scatter = [(low, high), (high, low)]
        rest = self.other + z_bits
        self.rest = list(zip(rest, rest[::-1]))
        self.replicas = list(zip(z_bits, z_bits[::-1]))
        self.low, self.high = low, high

    def send(self, x, step):
        pairs = []
        for d in range(self.dp):
            for m in range(self.mp):
                axis, bit = step[d % 2]
                to = (d ^ bit) * self.mp + m if axis == "dp" else d * self.mp + (m ^ bit)
                pairs.append((d * self.mp + m, to))
        return lax.ppermute(x, AXES, pairs)

    def core(self, x):
        return self.send(x, (("dp", 1), ("dp", 1)))


def on_device(dp, mp, grad, error, init):
    grad, error = grad[0], error[0]
    rows, cols = grad.shape
    rank = init.shape[1]
    net = Exchange(dp, mp)
    place = [lax.axis_index(axis).astype(jnp.int32).reshape(1) for axis in AXES]
    units = cols // 8 // LANES
    square = (rank, LANES)

    comp, near, far = left_product(net, place, grad, error, init)
    near = near + net.core(far)
    for step in net.replicas:
        sent = lax.reduce_precision(near, 8, 7)
        near = sent + net.send(sent.astype(BF16), step).astype(F32)
    near = near.astype(BF16)
    far = net.core(near)

    def right(side, places, dtype):
        return right_product(net, place, side, places, units, comp, near, far, dtype)

    def small(kernel, name, outs, *ins):
        return call(kernel, name, outs, [VMEM] * len(ins), 4, 0.3, out_specs=jax.tree.map(lambda _: VMEM, outs))(*ins)

    block, square_f32 = shaped((units, *square), BF16), shaped((rank, rank), F32)
    across_3 = net.core(right(FAR, (3,), BF16))
    across_2 = net.core(right(FAR, (2,), BF16))
    sent = small(add_kernel, "first_sum", block, right(NEAR, (3,), F32), across_3)
    near, far, sent = lax.optimization_barrier((near, far, sent))
    arrived_1 = net.send(sent, net.scatter[0])
    sent, gram = small(
        first_kernel, "first_sum", [shaped((units + 2, *square), BF16), square_f32],
        right(NEAR, (2,), F32), across_2, near, far,
    )
    near, far, sent = lax.optimization_barrier((near, far, sent))
    arrived_0 = net.send(sent, net.scatter[0])
    across = net.core(right(FAR, (1,), BF16))
    part = right(NEAR, (1,), F32)
    near, far, arrived_1 = lax.optimization_barrier((near, far, arrived_1))
    sent = small(second_kernel, "second_sum", block, part, across, arrived_1)
    across = net.core(right(FAR, (0,), BF16))
    part = right(NEAR, (0,), F32)
    arrived = net.send(sent, net.scatter[1])
    kept, gram = small(
        kept_kernel, "second_sum", [shaped((units, *square), F32), square_f32], part, across, arrived_0, gram
    )
    gram = gram + net.send(gram, net.scatter[1])
    for bit in net.other:
        gram = gram + net.send(gram, (bit, bit))
    sent = small(add_kernel, "third_sum", block, kept, arrived)

    for step in net.rest[:-1]:
        arrived, gram = lax.optimization_barrier((net.send(sent, step), gram))
        sent = small(add_kernel, "pair_sum", block, sent, arrived)
    arrived = net.send(sent, net.rest[-1])
    sent, gram = lax.optimization_barrier((sent, gram))
    state = inverse_of(gram)
    base_near, base_far = small(base_kernel, "base", [shaped((rows // 2, rank), BF16)] * 2, near, far, state)
    arrived, state, base_near, base_far = lax.optimization_barrier((arrived, state, base_near, base_far))
    own = small(functools.partial(factor_kernel, dp), "factor", block, sent, arrived, state)

    blocks = [own, net.send(own, net.scatter[1]), net.send(own, net.scatter[0]), None]
    write = functools.partial(new_error, net, place, units=units, comp=comp, near=base_near, far=base_far)
    out = write([(NEAR, 0)], [own])
    own, out = lax.optimization_barrier((own, out))
    others = [net.core(own)]
    blocks[1], out = lax.optimization_barrier((blocks[1], out))
    blocks[3] = net.send(blocks[1], net.scatter[0])
    others.append(net.core(blocks[1]))
    blocks[2], out = lax.optimization_barrier((blocks[2], out))
    others.append(net.core(blocks[2]))
    share, width = cols // mp, units * LANES
    right_factor = None
    some = [(FAR, 0), (NEAR, 1), (FAR, 1)], [others[0], blocks[1], others[1]]
    if share == 2 * width:
        out, right_factor = write(*some, held=out, own=own)
    else:
        out = write(*some, held=out)
    blocks[3], out = lax.optimization_barrier((blocks[3], out))
    others.append(net.core(blocks[3]))
    out = write([(NEAR, 2), (FAR, 2)], [blocks[2], others[2]], held=out)
    out = write([(NEAR, 3), (FAR, 3)], [blocks[3], others[3]], held=out)
    if right_factor is None:
        everything = jnp.concatenate(blocks + others, axis=0)
        here = Place(net, place)
        names = jnp.stack([here.block(side, k) for side in (NEAR, FAR) for k in range(4)])
        block = here.mp * share // width
        chosen = lax.dynamic_slice_in_dim(everything, jnp.argmax(names == block) * units, units, 0)
        chosen = jnp.swapaxes(chosen, 1, 2).reshape(width, rank)
        right_factor = lax.dynamic_slice_in_dim(chosen, here.mp * share - block * width, share, 0)
    return (out[None], right_factor)


def solution(mesh):
    return jax.shard_map(
        functools.partial(on_device, mesh.shape["dp"], mesh.shape["mp"]),
        mesh=mesh,
        in_specs=(P("dp", "mp", None), P("dp", "mp", None), P()),
        out_specs=(P("dp", "mp", None), P("mp", None)),
        check_vma=False,
    )
```

```python
import functools

import jax
import jax.numpy as jnp
from jax import lax
from jax.experimental import pallas as pl
from jax.experimental.pallas import tpu as pltpu
from jax.sharding import PartitionSpec as P

F32 = jnp.float32
BF16 = jnp.bfloat16
LANES = 128
MIB = 1024 * 1024
AXES = ("dp", "mp")
PIECES = 14
LEAF = 8

VMEM = pl.BlockSpec(memory_space=pltpu.VMEM)
HBM = pl.BlockSpec(memory_space=pltpu.HBM)
SMEM = pl.BlockSpec(memory_space=pltpu.SMEM)

NEAR, FAR = 0, 1


class Place:
    def __init__(self, net, place):
        self.net = net
        self.dp, self.mp = place[0][0], place[1][0]
        self.core = self.dp & 1

    def half(self, side):
        return self.core if side == NEAR else 1 - self.core

    def bit(self, name):
        axis, value = name
        return ((self.dp if axis == "dp" else self.mp) >> (value.bit_length() - 1)) & 1

    def block(self, side, k):
        core = self.half(side)
        a, b = k // 2, k % 2
        low = self.bit(self.net.low) ^ (a + (b - a) * core)
        high = self.bit(self.net.high) ^ (b + (a - b) * core)
        return high * 4 + low * 2 + core


def call(kernel, name, outs, ins, vmem_mib, micros, **more):
    return pl.pallas_call(
        kernel,
        out_shape=outs,
        in_specs=ins,
        compiler_params=pltpu.CompilerParams(vmem_limit_bytes=vmem_mib * MIB),
        cost_estimate=pl.CostEstimate(flops=0, bytes_accessed=int(micros * 3.5e6), transcendentals=0),
        name=name,
        **more,
    )


def shaped(shape, dtype):
    return jax.ShapeDtypeStruct(shape, dtype)


def in_hbm(x):
    return pltpu.with_memory_space_constraint(x, pltpu.HBM)


def in_vmem(x):
    return pltpu.with_memory_space_constraint(x, pltpu.VMEM)


def left_kernel(net, pieces, dp, mp, grad, error, init, comp, near, far, error_v, init_v, sems):
    place = Place(net, (dp, mp))
    rows, cols = comp.shape
    count, width = rows // 2, cols // pieces

    def copies(i):
        at = pl.ds(i * width, width)
        out = [pltpu.make_async_copy(init.at[at], init_v.at[at], sems.at[4, i])]
        for half in range(2):
            source = pl.ds(pl.multiple_of(place.half(half) * count, count), count)
            target = pl.ds(half * count, count)
            out.append(pltpu.make_async_copy(grad.at[source, at], comp.at[target, at], sems.at[half, i]))
            out.append(pltpu.make_async_copy(error.at[source, at], error_v.at[target, at], sems.at[2 + half, i]))
        return out

    for i in range(pieces):
        for copy in copies(i):
            copy.start()
    for i in range(pieces):
        for copy in copies(i):
            copy.wait()
        at = pl.ds(i * width, width)
        total = (comp[:, at].astype(F32) + error_v[:, at].astype(F32)).astype(BF16)
        comp[:, at] = total
        part = lax.dot_general(init_v[at].T, total, (((1,), (1,)), ((), ())), preferred_element_type=F32)
        if i == 0:
            near[...] = part[:, :count]
            far[...] = part[:, count:]
        else:
            near[...] += part[:, :count]
            far[...] += part[:, count:]


def left_product(net, place, grad, error, init):
    rows, cols = grad.shape
    rank = init.shape[1]
    return call(
        functools.partial(left_kernel, net, PIECES),
        "left_product",
        [pltpu.VMEM((rows, cols), BF16), shaped((rank, rows // 2), F32), shaped((rank, rows // 2), F32)],
        [SMEM, SMEM, HBM, HBM, HBM],
        26,
        12,
        out_specs=[VMEM] * 3,
        scratch_shapes=[
            pltpu.VMEM((rows, cols), BF16),
            pltpu.VMEM((cols, rank), BF16),
            pltpu.SemaphoreType.DMA((5, PIECES)),
        ],
    )(*place, in_hbm(grad), in_hbm(error), in_hbm(init))


def right_kernel(net, units, side, places, dp, mp, comp, near, far, out):
    place = Place(net, (dp, mp))
    rows = comp.shape[0]
    count = rows // 2
    for block, k in enumerate(places):
        start = place.block(side, k) * (units * LANES)
        for unit in range(0, units, 2):
            wide = min(2, units - unit)
            at = pl.ds(pl.multiple_of(start + unit * LANES, LANES), wide * LANES)
            product = jnp.dot(near[...], comp[:count, at], preferred_element_type=F32)
            product += jnp.dot(far[...], comp[count:, at], preferred_element_type=F32)
            for k in range(wide):
                out[block * units + unit + k] = product[:, k * LANES : (k + 1) * LANES].astype(out.dtype)


def right_product(net, place, side, places, units, comp, near, far, dtype):
    rank = near.shape[0]
    return call(
        functools.partial(right_kernel, net, units, side, places),
        "right_product",
        shaped((len(places) * units, rank, LANES), dtype),
        [SMEM, SMEM, VMEM, VMEM, VMEM],
        4,
        0.7 * len(places),
        out_specs=VMEM,
    )(*place, in_vmem(comp), near, far)


def new_error_kernel(net, units, blocks, rows_too, dp, mp, comp, near, far, *rest):
    place = Place(net, (dp, mp))
    rights, rest = rest[: len(blocks)], rest[len(blocks) :]
    count = comp.shape[0] // 2
    copies = []
    if rows_too:
        own, other, _, out, factor_rows, buf, sems, rows_buf, rows_sem = rest
        for side, source in ((NEAR, own), (FAR, other)):
            start = place.half(side) * (units * LANES)
            for i in range(units):
                rows_buf[pl.ds(pl.multiple_of(start + i * LANES, LANES), LANES), :] = source[i].T
        copies.append(pltpu.make_async_copy(rows_buf, factor_rows, rows_sem))
        copies[0].start()
    else:
        out, buf, sems = rest[-3:]
    step = min(128, count)
    for j, ((side, k), right) in enumerate(zip(blocks, rights)):
        start = place.block(side, k) * (units * LANES)
        for half, base in enumerate((near, far)):
            rows = pl.ds(pl.multiple_of(place.half(half) * count, count), count)
            for unit in range(0, units, 2):
                wide = min(2, units - unit)
                factor = [right[unit + i] for i in range(wide)]
                factor = jnp.concatenate(factor, axis=1) if wide > 1 else factor[0]
                at = pl.ds(pl.multiple_of(start + unit * LANES, LANES), wide * LANES)
                here = pl.ds(unit * LANES, wide * LANES)
                for row in range(0, count, step):
                    product = jnp.dot(base[row : row + step], factor, preferred_element_type=F32)
                    kept = comp[half * count + row : half * count + row + step, at].astype(F32)
                    buf[half, j, row : row + step, here] = (kept - product).astype(BF16)
                copy = pltpu.make_async_copy(
                    buf.at[half, j, :, here], out.at[rows, at], sems.at[half, j, unit // 2]
                )
                copy.start()
                copies.append(copy)
    for copy in copies:
        copy.wait()


def new_error(net, place, blocks, rights, units, comp, near, far, held=None, block_0=()):
    rows, cols = comp.shape
    rank = near.shape[1]
    outs, scratch = [shaped((rows, cols), BF16)], [
        pltpu.VMEM((2, len(blocks), rows // 2, units * LANES), BF16),
        pltpu.SemaphoreType.DMA((2, len(blocks), (units + 1) // 2)),
    ]
    if block_0:
        outs.append(shaped((2 * units * LANES, rank), BF16))
        scratch += [pltpu.VMEM((2 * units * LANES, rank), BF16), pltpu.SemaphoreType.DMA]
    held = [] if held is None else [in_hbm(held)]
    out = call(
        functools.partial(new_error_kernel, net, units, blocks, len(block_0)),
        "new_error",
        outs,
        [SMEM] * 2 + [VMEM] * (3 + len(blocks) + len(block_0)) + [HBM] * len(held),
        12,
        0.6 + 0.8 * len(blocks),
        out_specs=[HBM] * len(outs),
        scratch_shapes=scratch,
        input_output_aliases={5 + len(blocks) + len(block_0): 0} if held else {},
    )(*place, in_vmem(comp), near, far, *rights, *block_0, *held)
    return out if block_0 else out[0]


def leaf_steps(state, leaf):
    n, b = state.shape[0], LEAF
    base = leaf * b

    def splat(v):
        return jnp.broadcast_to(v, (b, n))

    def column(tile, j):
        return splat(state[b * tile : b * tile + b, base + j : base + j + 1])

    here = [column(leaf, j) for j in range(b)]
    a = [[splat(here[j][i : i + 1]) if j <= i else None for j in range(b)] for i in range(b)]
    mult = [[None] * b for _ in range(b)]
    unit = [[None] * b for _ in range(b)]
    recip, scale = [], []
    for k in range(b):
        recip.append(1.0 / a[k][k])
        scale.append(lax.rsqrt(a[k][k]))
        for i in range(k + 1, b):
            mult[i][k] = a[i][k] * recip[k]
        for i in range(k + 1, b):
            for j in range(k + 1, i + 1):
                a[i][j] = a[i][j] - mult[i][k] * a[j][k]
    for j in range(b):
        for i in range(j + 1, b):
            total = mult[i][j]
            for k in range(j + 1, i):
                total = total + mult[i][k] * unit[k][j]
            unit[i][j] = -total
    rows_x = [splat(state[base + j : base + j + 1, n:]) for j in range(b)]
    if leaf + 1 < n // b:
        rows_g = [splat(state[base + j : base + j + 1, :n]) for j in range(b)]

        def term(k, j):
            return recip[k] if j == k else recip[k] * unit[k][j]

        inverse = [[None] * b for _ in range(b)]
        for i in range(b):
            for j in range(i + 1):
                total = term(i, j)
                for k in range(i + 1, b):
                    total = total + unit[k][i] * term(k, j)
                inverse[i][j] = inverse[j][i] = total

        def mixed(rows):
            out = []
            for k in range(b):
                total = inverse[k][0] * rows[0]
                for j in range(1, b):
                    total = total + inverse[k][j] * rows[j]
                out.append(total)
            return out

        mixed_g, mixed_x = mixed(rows_g), mixed(rows_x)
        for tile in range(leaf + 1, n // b):
            at = slice(b * tile, b * tile + b)
            columns = [column(tile, j) for j in range(b)]
            g, x = state[at, :n], state[at, n:]
            for k in range(b):
                g = g - columns[k] * mixed_g[k]
                x = x - columns[k] * mixed_x[k]
            state[at, :n] = g
            state[at, n:] = x
    for i in range(b):
        total = rows_x[i]
        for j in range(i):
            total = total + unit[i][j] * rows_x[j]
        state[base + i : base + i + 1, n:] = (total * scale[i])[:1]


def inverse_kernel(gram, state):
    n = state.shape[0]
    state[:, :n] = gram[...]
    row = lax.broadcasted_iota(jnp.int32, (n, n), 0)
    state[:, n:] = (row == lax.broadcasted_iota(jnp.int32, (n, n), 1)).astype(F32)
    for leaf in range(n // LEAF):
        leaf_steps(state, leaf)


def inverse_of(gram):
    n = gram.shape[0]
    return call(inverse_kernel, "inverse", shaped((n, 2 * n), F32), [VMEM], 4, 4.5, out_specs=VMEM)(gram)


def split2(x):
    high = x.astype(BF16)
    return high, (x - high.astype(F32)).astype(BF16)


def first_kernel(part, across, near, far, out, gram):
    units = part.shape[0]
    contract = (((1,), (1,)), ((), ()))
    total = lax.dot_general(near[...], near[...], contract, preferred_element_type=F32)
    total += lax.dot_general(far[...], far[...], contract, preferred_element_type=F32)
    out[units], out[units + 1] = split2(total)
    gram[...] = out[units].astype(F32) + out[units + 1].astype(F32)
    for i in range(units):
        out[i] = (part[i] + across[i].astype(F32)).astype(BF16)


def second_kernel(part, across, arrived, out):
    for i in range(out.shape[0]):
        out[i] = (part[i] + across[i].astype(F32) + arrived[i].astype(F32)).astype(BF16)


def kept_kernel(part, across, arrived, gram_in, out, gram):
    units = out.shape[0]
    gram[...] = gram_in[...] + (arrived[units].astype(F32) + arrived[units + 1].astype(F32))
    for i in range(units):
        out[i] = part[i] + across[i].astype(F32) + arrived[i].astype(F32)


def add_kernel(one, other, out):
    for i in range(one.shape[0]):
        out[i] = (one[i].astype(F32) + other[i].astype(F32)).astype(BF16)


def factor_kernel(replicas, own, arrived, state, out):
    units, rank = own.shape[:2]
    lhs = jnp.concatenate(split2(state[:, rank:]), axis=0)
    for i in range(0, units, 2):
        some = range(i, min(i + 2, units))
        summed = [(own[k].astype(F32) + arrived[k].astype(F32)).astype(BF16) for k in some]
        summed = jnp.concatenate(summed, axis=1) if len(summed) > 1 else summed[0]
        product = jnp.dot(lhs, summed, preferred_element_type=F32)
        product = (product[:rank] + product[rank:]) / replicas
        for k in some:
            out[k] = product[:, (k - i) * LANES : (k - i + 1) * LANES].astype(BF16)


def base_kernel(near, far, state, near_out, far_out):
    rank = near.shape[0]
    lhs = jnp.concatenate(split2(state[:, rank:]), axis=0)
    for source, out in ((near, near_out), (far, far_out)):
        product = jnp.dot(lhs, source[...], preferred_element_type=F32)
        out[...] = (product[:rank] + product[rank:]).T.astype(BF16)


class Exchange:
    def __init__(self, dp, mp):
        self.dp, self.mp = dp, mp
        mp_bits = [("mp", 1 << k) for k in range(mp.bit_length() - 1)]
        z_bits = [("dp", 2 << k) for k in range(dp.bit_length() - 2)]
        low, high = mp_bits[0], mp_bits[len(mp_bits) // 2]
        self.other = [bit for bit in mp_bits if bit not in (low, high)]
        self.scatter = [(low, high), (high, low)]
        rest = self.other + z_bits
        self.rest = list(zip(rest, rest[::-1]))
        self.replicas = list(zip(z_bits, z_bits[::-1]))
        self.low, self.high = low, high

    def send(self, x, step):
        pairs = []
        for d in range(self.dp):
            for m in range(self.mp):
                axis, bit = step[d % 2]
                to = (d ^ bit) * self.mp + m if axis == "dp" else d * self.mp + (m ^ bit)
                pairs.append((d * self.mp + m, to))
        return lax.ppermute(x, AXES, pairs)

    def core(self, x):
        return self.send(x, (("dp", 1), ("dp", 1)))


def on_device(dp, mp, grad, error, init):
    grad, error = grad[0], error[0]
    rows, cols = grad.shape
    rank = init.shape[1]
    net = Exchange(dp, mp)
    place = [lax.axis_index(axis).astype(jnp.int32).reshape(1) for axis in AXES]
    units = cols // 8 // LANES
    square = (rank, LANES)

    comp, near, far = left_product(net, place, grad, error, init)
    near = near + net.core(far)
    for step in net.replicas:
        sent = lax.reduce_precision(near, 8, 7)
        near = sent + net.send(sent.astype(BF16), step).astype(F32)
    near = near.astype(BF16)
    far = net.core(near)

    def right(side, places, dtype):
        return right_product(net, place, side, places, units, comp, near, far, dtype)

    def small(kernel, name, outs, *ins):
        return call(kernel, name, outs, [VMEM] * len(ins), 4, 0.3, out_specs=jax.tree.map(lambda _: VMEM, outs))(*ins)

    block, square_f32 = shaped((units, *square), BF16), shaped((rank, rank), F32)
    across_3 = net.core(right(FAR, (3,), BF16))
    across_2 = net.core(right(FAR, (2,), BF16))
    sent = small(add_kernel, "first_sum", block, right(NEAR, (3,), F32), across_3)
    near, far, sent = lax.optimization_barrier((near, far, sent))
    arrived_1 = net.send(sent, net.scatter[0])
    sent, gram = small(
        first_kernel, "first_sum", [shaped((units + 2, *square), BF16), square_f32],
        right(NEAR, (2,), F32), across_2, near, far,
    )
    near, far, sent = lax.optimization_barrier((near, far, sent))
    arrived_0 = net.send(sent, net.scatter[0])
    across = net.core(right(FAR, (1,), BF16))
    part = right(NEAR, (1,), F32)
    near, far, arrived_1 = lax.optimization_barrier((near, far, arrived_1))
    sent = small(second_kernel, "second_sum", block, part, across, arrived_1)
    across = net.core(right(FAR, (0,), BF16))
    part = right(NEAR, (0,), F32)
    arrived = net.send(sent, net.scatter[1])
    kept, gram = small(
        kept_kernel, "second_sum", [shaped((units, *square), F32), square_f32], part, across, arrived_0, gram
    )
    gram = gram + net.send(gram, net.scatter[1])
    for bit in net.other:
        gram = gram + net.send(gram, (bit, bit))
    sent = small(add_kernel, "third_sum", block, kept, arrived)

    for step in net.rest[:-1]:
        arrived, gram = lax.optimization_barrier((net.send(sent, step), gram))
        sent = small(add_kernel, "pair_sum", block, sent, arrived)
    arrived = net.send(sent, net.rest[-1])
    sent, gram = lax.optimization_barrier((sent, gram))
    state = inverse_of(gram)
    base_near, base_far = small(base_kernel, "base", [shaped((rows // 2, rank), BF16)] * 2, near, far, state)
    arrived, state, base_near, base_far = lax.optimization_barrier((arrived, state, base_near, base_far))
    own = small(functools.partial(factor_kernel, dp), "factor", block, sent, arrived, state)

    blocks = [own, net.send(own, net.scatter[1]), net.send(own, net.scatter[0]), None]
    write = functools.partial(new_error, net, place, units=units, comp=comp, near=base_near, far=base_far)
    out = write([(NEAR, 0)], [own])
    own, out = lax.optimization_barrier((own, out))
    others = [net.core(own)]
    blocks[1], out = lax.optimization_barrier((blocks[1], out))
    blocks[3] = net.send(blocks[1], net.scatter[0])
    others.append(net.core(blocks[1]))
    blocks[2], out = lax.optimization_barrier((blocks[2], out))
    others.append(net.core(blocks[2]))
    share, width = cols // mp, units * LANES
    right_factor = None
    some = [(FAR, 0), (NEAR, 1), (FAR, 1), (NEAR, 2)], [others[0], blocks[1], others[1], blocks[2]]
    if share == 2 * width:
        out, right_factor = write(*some, held=out, block_0=(own, others[0]))
    else:
        out = write(*some, held=out)
    blocks[3], out = lax.optimization_barrier((blocks[3], out))
    others.append(net.core(blocks[3]))
    out = write([(FAR, 2), (NEAR, 3)], [others[2], blocks[3]], held=out)
    out = write([(FAR, 3)], [others[3]], held=out)
    if right_factor is None:
        everything = jnp.concatenate(blocks + others, axis=0)
        here = Place(net, place)
        names = jnp.stack([here.block(side, k) for side in (NEAR, FAR) for k in range(4)])
        block = here.mp * share // width
        chosen = lax.dynamic_slice_in_dim(everything, jnp.argmax(names == block) * units, units, 0)
        chosen = jnp.swapaxes(chosen, 1, 2).reshape(width, rank)
        right_factor = lax.dynamic_slice_in_dim(chosen, here.mp * share - block * width, share, 0)
    return (out[None], right_factor)


def solution(mesh):
    return jax.shard_map(
        functools.partial(on_device, mesh.shape["dp"], mesh.shape["mp"]),
        mesh=mesh,
        in_specs=(P("dp", "mp", None), P("dp", "mp", None), P()),
        out_specs=(P("dp", "mp", None), P("mp", None)),
        check_vma=False,
    )
```

```python
import functools

import jax
import jax.numpy as jnp
from jax import lax
from jax.experimental import pallas as pl
from jax.experimental.pallas import tpu as pltpu
from jax.sharding import PartitionSpec as P

F32 = jnp.float32
BF16 = jnp.bfloat16
LANES = 128
MIB = 1024 * 1024
AXES = ("dp", "mp")
PIECES = 14
LEAF = 8

VMEM = pl.BlockSpec(memory_space=pltpu.VMEM)
HBM = pl.BlockSpec(memory_space=pltpu.HBM)
SMEM = pl.BlockSpec(memory_space=pltpu.SMEM)

NEAR, FAR = 0, 1


class Place:
    def __init__(self, net, place):
        self.net = net
        self.dp, self.mp = place[0][0], place[1][0]
        self.core = self.dp & 1

    def half(self, side):
        return self.core if side == NEAR else 1 - self.core

    def bit(self, name):
        axis, value = name
        return ((self.dp if axis == "dp" else self.mp) >> (value.bit_length() - 1)) & 1

    def block(self, side, k):
        core = self.half(side)
        a, b = k // 2, k % 2
        low = self.bit(self.net.low) ^ (a + (b - a) * core)
        high = self.bit(self.net.high) ^ (b + (a - b) * core)
        return high * 4 + low * 2 + core


def call(kernel, name, outs, ins, vmem_mib, micros, **more):
    return pl.pallas_call(
        kernel,
        out_shape=outs,
        in_specs=ins,
        compiler_params=pltpu.CompilerParams(vmem_limit_bytes=vmem_mib * MIB),
        cost_estimate=pl.CostEstimate(flops=0, bytes_accessed=int(micros * 3.5e6), transcendentals=0),
        name=name,
        **more,
    )


def shaped(shape, dtype):
    return jax.ShapeDtypeStruct(shape, dtype)


def in_hbm(x):
    return pltpu.with_memory_space_constraint(x, pltpu.HBM)


def in_vmem(x):
    return pltpu.with_memory_space_constraint(x, pltpu.VMEM)


def left_kernel(net, pieces, dp, mp, grad, error, init, comp, near, far, error_v, init_v, sems):
    place = Place(net, (dp, mp))
    rows, cols = comp.shape
    count, width = rows // 2, cols // pieces

    def copies(i):
        at = pl.ds(i * width, width)
        out = [pltpu.make_async_copy(init.at[at], init_v.at[at], sems.at[4, i])]
        for half in range(2):
            source = pl.ds(pl.multiple_of(place.half(half) * count, count), count)
            target = pl.ds(half * count, count)
            out.append(pltpu.make_async_copy(grad.at[source, at], comp.at[target, at], sems.at[half, i]))
            out.append(pltpu.make_async_copy(error.at[source, at], error_v.at[target, at], sems.at[2 + half, i]))
        return out

    for i in range(pieces):
        for copy in copies(i):
            copy.start()
    for i in range(pieces):
        for copy in copies(i):
            copy.wait()
        at = pl.ds(i * width, width)
        total = (comp[:, at].astype(F32) + error_v[:, at].astype(F32)).astype(BF16)
        comp[:, at] = total
        part = lax.dot_general(init_v[at].T, total, (((1,), (1,)), ((), ())), preferred_element_type=F32)
        if i == 0:
            near[...] = part[:, :count]
            far[...] = part[:, count:]
        else:
            near[...] += part[:, :count]
            far[...] += part[:, count:]


def left_product(net, place, grad, error, init):
    rows, cols = grad.shape
    rank = init.shape[1]
    return call(
        functools.partial(left_kernel, net, PIECES),
        "left_product",
        [pltpu.VMEM((rows, cols), BF16), shaped((rank, rows // 2), F32), shaped((rank, rows // 2), F32)],
        [SMEM, SMEM, HBM, HBM, HBM],
        26,
        12,
        out_specs=[VMEM] * 3,
        scratch_shapes=[
            pltpu.VMEM((rows, cols), BF16),
            pltpu.VMEM((cols, rank), BF16),
            pltpu.SemaphoreType.DMA((5, PIECES)),
        ],
    )(*place, in_hbm(grad), in_hbm(error), in_hbm(init))


def right_kernel(net, units, side, places, dp, mp, comp, near, far, out):
    place = Place(net, (dp, mp))
    rows = comp.shape[0]
    count = rows // 2
    for block, k in enumerate(places):
        start = place.block(side, k) * (units * LANES)
        for unit in range(0, units, 2):
            wide = min(2, units - unit)
            at = pl.ds(pl.multiple_of(start + unit * LANES, LANES), wide * LANES)
            product = jnp.dot(near[...], comp[:count, at], preferred_element_type=F32)
            product += jnp.dot(far[...], comp[count:, at], preferred_element_type=F32)
            for k in range(wide):
                out[block * units + unit + k] = product[:, k * LANES : (k + 1) * LANES].astype(out.dtype)


def right_product(net, place, side, places, units, comp, near, far, dtype):
    rank = near.shape[0]
    return call(
        functools.partial(right_kernel, net, units, side, places),
        "right_product",
        shaped((len(places) * units, rank, LANES), dtype),
        [SMEM, SMEM, VMEM, VMEM, VMEM],
        4,
        0.7 * len(places),
        out_specs=VMEM,
    )(*place, in_vmem(comp), near, far)


def new_error_kernel(net, units, blocks, rows_too, dp, mp, comp, near, far, *rest):
    place = Place(net, (dp, mp))
    rights, rest = rest[: len(blocks)], rest[len(blocks) :]
    count = comp.shape[0] // 2
    copies = []
    if rows_too:
        own, other, _, out, factor_rows, buf, sems, rows_buf, rows_sem = rest
        for side, source in ((NEAR, own), (FAR, other)):
            start = place.half(side) * (units * LANES)
            for i in range(units):
                rows_buf[pl.ds(pl.multiple_of(start + i * LANES, LANES), LANES), :] = source[i].T
        copies.append(pltpu.make_async_copy(rows_buf, factor_rows, rows_sem))
        copies[0].start()
    else:
        out, buf, sems = rest[-3:]
    step = min(128, count)
    for j, ((side, k), right) in enumerate(zip(blocks, rights)):
        start = place.block(side, k) * (units * LANES)
        for half, base in enumerate((near, far)):
            rows = pl.ds(pl.multiple_of(place.half(half) * count, count), count)
            for unit in range(0, units, 2):
                wide = min(2, units - unit)
                factor = [right[unit + i] for i in range(wide)]
                factor = jnp.concatenate(factor, axis=1) if wide > 1 else factor[0]
                at = pl.ds(pl.multiple_of(start + unit * LANES, LANES), wide * LANES)
                here = pl.ds(unit * LANES, wide * LANES)
                for row in range(0, count, step):
                    product = jnp.dot(base[row : row + step], factor, preferred_element_type=F32)
                    kept = comp[half * count + row : half * count + row + step, at].astype(F32)
                    buf[half, j, row : row + step, here] = (kept - product).astype(BF16)
                copy = pltpu.make_async_copy(
                    buf.at[half, j, :, here], out.at[rows, at], sems.at[half, j, unit // 2]
                )
                copy.start()
                copies.append(copy)
    for copy in copies:
        copy.wait()


def new_error(net, place, blocks, rights, units, comp, near, far, held=None, block_0=()):
    rows, cols = comp.shape
    rank = near.shape[1]
    outs, scratch = [shaped((rows, cols), BF16)], [
        pltpu.VMEM((2, len(blocks), rows // 2, units * LANES), BF16),
        pltpu.SemaphoreType.DMA((2, len(blocks), (units + 1) // 2)),
    ]
    if block_0:
        outs.append(shaped((2 * units * LANES, rank), BF16))
        scratch += [pltpu.VMEM((2 * units * LANES, rank), BF16), pltpu.SemaphoreType.DMA]
    held = [] if held is None else [in_hbm(held)]
    out = call(
        functools.partial(new_error_kernel, net, units, blocks, len(block_0)),
        "new_error",
        outs,
        [SMEM] * 2 + [VMEM] * (3 + len(blocks) + len(block_0)) + [HBM] * len(held),
        12,
        0.6 + 0.8 * len(blocks),
        out_specs=[HBM] * len(outs),
        scratch_shapes=scratch,
        input_output_aliases={5 + len(blocks) + len(block_0): 0} if held else {},
    )(*place, in_vmem(comp), near, far, *rights, *block_0, *held)
    return out if block_0 else out[0]


def leaf_steps(state, leaf):
    n, b = state.shape[0], LEAF
    base = leaf * b

    def splat(v):
        return jnp.broadcast_to(v, (b, n))

    def column(tile, j):
        return splat(state[b * tile : b * tile + b, base + j : base + j + 1])

    here = [column(leaf, j) for j in range(b)]
    a = [[splat(here[j][i : i + 1]) if j <= i else None for j in range(b)] for i in range(b)]
    mult = [[None] * b for _ in range(b)]
    unit = [[None] * b for _ in range(b)]
    recip, scale = [], []
    for k in range(b):
        recip.append(1.0 / a[k][k])
        scale.append(lax.rsqrt(a[k][k]))
        for i in range(k + 1, b):
            mult[i][k] = a[i][k] * recip[k]
        for i in range(k + 1, b):
            for j in range(k + 1, i + 1):
                a[i][j] = a[i][j] - mult[i][k] * a[j][k]
    for j in range(b):
        for i in range(j + 1, b):
            total = mult[i][j]
            for k in range(j + 1, i):
                total = total + mult[i][k] * unit[k][j]
            unit[i][j] = -total
    rows_x = [splat(state[base + j : base + j + 1, n:]) for j in range(b)]
    if leaf + 1 < n // b:
        rows_g = [splat(state[base + j : base + j + 1, :n]) for j in range(b)]

        def term(k, j):
            return recip[k] if j == k else recip[k] * unit[k][j]

        inverse = [[None] * b for _ in range(b)]
        for i in range(b):
            for j in range(i + 1):
                total = term(i, j)
                for k in range(i + 1, b):
                    total = total + unit[k][i] * term(k, j)
                inverse[i][j] = inverse[j][i] = total

        def mixed(rows):
            out = []
            for k in range(b):
                total = inverse[k][0] * rows[0]
                for j in range(1, b):
                    total = total + inverse[k][j] * rows[j]
                out.append(total)
            return out

        mixed_g, mixed_x = mixed(rows_g), mixed(rows_x)
        for tile in range(leaf + 1, n // b):
            at = slice(b * tile, b * tile + b)
            columns = [column(tile, j) for j in range(b)]
            g, x = state[at, :n], state[at, n:]
            for k in range(b):
                g = g - columns[k] * mixed_g[k]
                x = x - columns[k] * mixed_x[k]
            state[at, :n] = g
            state[at, n:] = x
    for i in range(b):
        total = rows_x[i]
        for j in range(i):
            total = total + unit[i][j] * rows_x[j]
        state[base + i : base + i + 1, n:] = (total * scale[i])[:1]


def inverse_kernel(gram, state):
    n = state.shape[0]
    state[:, :n] = gram[...]
    row = lax.broadcasted_iota(jnp.int32, (n, n), 0)
    state[:, n:] = (row == lax.broadcasted_iota(jnp.int32, (n, n), 1)).astype(F32)
    for leaf in range(n // LEAF):
        leaf_steps(state, leaf)


def inverse_of(gram):
    n = gram.shape[0]
    return call(inverse_kernel, "inverse", shaped((n, 2 * n), F32), [VMEM], 4, 4.5, out_specs=VMEM)(gram)


def split2(x):
    high = x.astype(BF16)
    return high, (x - high.astype(F32)).astype(BF16)


def gram_kernel(near, far, gram):
    contract = (((1,), (1,)), ((), ()))
    total = lax.dot_general(near[...], near[...], contract, preferred_element_type=F32)
    gram[...] = total + lax.dot_general(far[...], far[...], contract, preferred_element_type=F32)


def second_kernel(part, across, arrived, out):
    for i in range(out.shape[0]):
        out[i] = (part[i] + across[i].astype(F32) + arrived[i].astype(F32)).astype(BF16)


def kept_kernel(part, across, arrived, out):
    for i in range(out.shape[0]):
        out[i] = part[i] + across[i].astype(F32) + arrived[i].astype(F32)


def add_kernel(one, other, out):
    for i in range(one.shape[0]):
        out[i] = (one[i].astype(F32) + other[i].astype(F32)).astype(BF16)


def factor_kernel(replicas, one, other, out):
    for i in range(out.shape[0]):
        out[i] = ((one[i].astype(F32) + other[i].astype(F32)) / replicas).astype(BF16)


def base_kernel(near, far, state, near_out, far_out, near_rows, far_rows):
    rank = near.shape[0]
    lhs = jnp.concatenate(split2(state[:, rank:]), axis=0)
    for source, out, rows in ((near, near_out, near_rows), (far, far_out, far_rows)):
        product = jnp.dot(lhs, source[...], preferred_element_type=F32)
        product = product[:rank] + product[rank:]
        out[...] = product.astype(BF16)
        rows[...] = product.T.astype(BF16)


class Exchange:
    def __init__(self, dp, mp):
        self.dp, self.mp = dp, mp
        mp_bits = [("mp", 1 << k) for k in range(mp.bit_length() - 1)]
        z_bits = [("dp", 2 << k) for k in range(dp.bit_length() - 2)]
        low, high = mp_bits[0], mp_bits[len(mp_bits) // 2]
        other = [bit for bit in mp_bits if bit not in (low, high)]
        self.mp_bits = mp_bits
        self.scatter = [(low, high), (high, low)]
        rest = other + z_bits
        self.rest = list(zip(rest, rest[::-1]))
        self.replicas = list(zip(z_bits, z_bits[::-1]))
        self.low, self.high = low, high

    def send(self, x, step):
        pairs = []
        for d in range(self.dp):
            for m in range(self.mp):
                axis, bit = step[d % 2]
                to = (d ^ bit) * self.mp + m if axis == "dp" else d * self.mp + (m ^ bit)
                pairs.append((d * self.mp + m, to))
        return lax.ppermute(x, AXES, pairs)

    def core(self, x):
        return self.send(x, (("dp", 1), ("dp", 1)))


def on_device(dp, mp, grad, error, init):
    grad, error = grad[0], error[0]
    rows, cols = grad.shape
    rank = init.shape[1]
    net = Exchange(dp, mp)
    place = [lax.axis_index(axis).astype(jnp.int32).reshape(1) for axis in AXES]
    units = cols // 8 // LANES
    square = (rank, LANES)

    comp, near, far = left_product(net, place, grad, error, init)
    near = near + net.core(far)
    for step in net.replicas:
        sent = lax.reduce_precision(near, 8, 7)
        near = sent + net.send(sent.astype(BF16), step).astype(F32)
    near = near.astype(BF16)
    far = net.core(near)

    def small(kernel, name, outs, *ins):
        return call(kernel, name, outs, [VMEM] * len(ins), 4, 0.3, out_specs=jax.tree.map(lambda _: VMEM, outs))(*ins)

    gram = small(gram_kernel, "gram", shaped((rank, rank), F32), near, far)
    for bit in net.mp_bits:
        gram = gram + net.send(gram, (bit, bit))
    near, far, base_near, base_far = small(
        base_kernel, "base", [shaped((rank, rows // 2), BF16)] * 2 + [shaped((rows // 2, rank), BF16)] * 2,
        near, far, inverse_of(gram),
    )

    def right(side, places, dtype):
        return right_product(net, place, side, places, units, comp, near, far, dtype)

    block = shaped((units, *square), BF16)
    across_3 = net.core(right(FAR, (3,), BF16))
    across_2 = net.core(right(FAR, (2,), BF16))
    sent = small(add_kernel, "first_sum", block, right(NEAR, (3,), F32), across_3)
    near, far, sent = lax.optimization_barrier((near, far, sent))
    arrived_1 = net.send(sent, net.scatter[0])
    sent = small(add_kernel, "first_sum", block, right(NEAR, (2,), F32), across_2)
    near, far, sent = lax.optimization_barrier((near, far, sent))
    arrived_0 = net.send(sent, net.scatter[0])
    across = net.core(right(FAR, (1,), BF16))
    part = right(NEAR, (1,), F32)
    near, far, arrived_1 = lax.optimization_barrier((near, far, arrived_1))
    sent = small(second_kernel, "second_sum", block, part, across, arrived_1)
    across = net.core(right(FAR, (0,), BF16))
    part = right(NEAR, (0,), F32)
    arrived = net.send(sent, net.scatter[1])
    kept = small(kept_kernel, "second_sum", shaped((units, *square), F32), part, across, arrived_0)
    sent = small(add_kernel, "third_sum", block, kept, arrived)

    for step in net.rest[:-1]:
        sent = small(add_kernel, "pair_sum", block, sent, net.send(sent, step))
    arrived = net.send(sent, net.rest[-1])
    own = small(functools.partial(factor_kernel, dp), "factor", block, sent, arrived)

    blocks = [own, net.send(own, net.scatter[1]), net.send(own, net.scatter[0]), None]
    write = functools.partial(new_error, net, place, units=units, comp=comp, near=base_near, far=base_far)
    out = write([(NEAR, 0)], [own])
    own, out = lax.optimization_barrier((own, out))
    others = [net.core(own)]
    blocks[1], out = lax.optimization_barrier((blocks[1], out))
    blocks[3] = net.send(blocks[1], net.scatter[0])
    others.append(net.core(blocks[1]))
    blocks[2], out = lax.optimization_barrier((blocks[2], out))
    others.append(net.core(blocks[2]))
    share, width = cols // mp, units * LANES
    right_factor = None
    some = [(FAR, 0), (NEAR, 1), (FAR, 1), (NEAR, 2)], [others[0], blocks[1], others[1], blocks[2]]
    if share == 2 * width:
        out, right_factor = write(*some, held=out, block_0=(own, others[0]))
    else:
        out = write(*some, held=out)
    blocks[3], out = lax.optimization_barrier((blocks[3], out))
    others.append(net.core(blocks[3]))
    out = write([(FAR, 2), (NEAR, 3)], [others[2], blocks[3]], held=out)
    out = write([(FAR, 3)], [others[3]], held=out)
    if right_factor is None:
        everything = jnp.concatenate(blocks + others, axis=0)
        here = Place(net, place)
        names = jnp.stack([here.block(side, k) for side in (NEAR, FAR) for k in range(4)])
        block = here.mp * share // width
        chosen = lax.dynamic_slice_in_dim(everything, jnp.argmax(names == block) * units, units, 0)
        chosen = jnp.swapaxes(chosen, 1, 2).reshape(width, rank)
        right_factor = lax.dynamic_slice_in_dim(chosen, here.mp * share - block * width, share, 0)
    return (out[None], right_factor)


def solution(mesh):
    return jax.shard_map(
        functools.partial(on_device, mesh.shape["dp"], mesh.shape["mp"]),
        mesh=mesh,
        in_specs=(P("dp", "mp", None), P("dp", "mp", None), P()),
        out_specs=(P("dp", "mp", None), P("mp", None)),
        check_vma=False,
    )
```

```python
import functools

import jax
import jax.numpy as jnp
from jax import lax
from jax.experimental import pallas as pl
from jax.experimental.pallas import tpu as pltpu
from jax.sharding import PartitionSpec as P

F32 = jnp.float32
BF16 = jnp.bfloat16
LANES = 128
MIB = 1024 * 1024
AXES = ("dp", "mp")
PIECES = 7
LEAF = 8

VMEM = pl.BlockSpec(memory_space=pltpu.VMEM)
HBM = pl.BlockSpec(memory_space=pltpu.HBM)
SMEM = pl.BlockSpec(memory_space=pltpu.SMEM)

NEAR, FAR = 0, 1


class Place:
    def __init__(self, net, place):
        self.net = net
        self.dp, self.mp = place[0][0], place[1][0]
        self.core = self.dp & 1

    def half(self, side):
        return self.core if side == NEAR else 1 - self.core

    def bit(self, name):
        axis, value = name
        return ((self.dp if axis == "dp" else self.mp) >> (value.bit_length() - 1)) & 1

    def block(self, side, k):
        core = self.half(side)
        a, b = k // 2, k % 2
        low = self.bit(self.net.low) ^ (a + (b - a) * core)
        high = self.bit(self.net.high) ^ (b + (a - b) * core)
        return high * 4 + low * 2 + core


def call(kernel, name, outs, ins, vmem_mib, micros, **more):
    return pl.pallas_call(
        kernel,
        out_shape=outs,
        in_specs=ins,
        compiler_params=pltpu.CompilerParams(vmem_limit_bytes=vmem_mib * MIB),
        cost_estimate=pl.CostEstimate(flops=0, bytes_accessed=int(micros * 3.5e6), transcendentals=0),
        name=name,
        **more,
    )


def shaped(shape, dtype):
    return jax.ShapeDtypeStruct(shape, dtype)


def in_hbm(x):
    return pltpu.with_memory_space_constraint(x, pltpu.HBM)


def in_vmem(x):
    return pltpu.with_memory_space_constraint(x, pltpu.VMEM)


def left_kernel(net, pieces, dp, mp, grad, error, init, comp, near, far, error_v, init_v, sems):
    place = Place(net, (dp, mp))
    rows, cols = comp.shape
    count, width = rows // 2, cols // pieces

    def copies(i):
        at = pl.ds(i * width, width)
        out = [pltpu.make_async_copy(init.at[at], init_v.at[at], sems.at[4, i])]
        for half in range(2):
            source = pl.ds(pl.multiple_of(place.half(half) * count, count), count)
            target = pl.ds(half * count, count)
            out.append(pltpu.make_async_copy(grad.at[source, at], comp.at[target, at], sems.at[half, i]))
            out.append(pltpu.make_async_copy(error.at[source, at], error_v.at[target, at], sems.at[2 + half, i]))
        return out

    for i in range(pieces):
        for copy in copies(i):
            copy.start()
    for i in range(pieces):
        for copy in copies(i):
            copy.wait()
        at = pl.ds(i * width, width)
        total = (comp[:, at].astype(F32) + error_v[:, at].astype(F32)).astype(BF16)
        comp[:, at] = total
        part = lax.dot_general(init_v[at].T, total, (((1,), (1,)), ((), ())), preferred_element_type=F32)
        if i == 0:
            near[...] = part[:, :count]
            far[...] = part[:, count:]
        else:
            near[...] += part[:, :count]
            far[...] += part[:, count:]


def left_product(net, place, grad, error, init):
    rows, cols = grad.shape
    rank = init.shape[1]
    return call(
        functools.partial(left_kernel, net, PIECES),
        "left_product",
        [pltpu.VMEM((rows, cols), BF16), shaped((rank, rows // 2), F32), shaped((rank, rows // 2), F32)],
        [SMEM, SMEM, HBM, HBM, HBM],
        26,
        12,
        out_specs=[VMEM] * 3,
        scratch_shapes=[
            pltpu.VMEM((rows, cols), BF16),
            pltpu.VMEM((cols, rank), BF16),
            pltpu.SemaphoreType.DMA((5, PIECES)),
        ],
    )(*place, in_hbm(grad), in_hbm(error), in_hbm(init))


def right_kernel(net, units, side, places, dp, mp, comp, near, far, out):
    place = Place(net, (dp, mp))
    rows = comp.shape[0]
    count = rows // 2
    for block, k in enumerate(places):
        start = place.block(side, k) * (units * LANES)
        for unit in range(0, units, 2):
            wide = min(2, units - unit)
            at = pl.ds(pl.multiple_of(start + unit * LANES, LANES), wide * LANES)
            product = jnp.dot(near[...], comp[:count, at], preferred_element_type=F32)
            product += jnp.dot(far[...], comp[count:, at], preferred_element_type=F32)
            for k in range(wide):
                out[block * units + unit + k] = product[:, k * LANES : (k + 1) * LANES].astype(out.dtype)


def right_product(net, place, side, places, units, comp, near, far, dtype):
    rank = near.shape[0]
    return call(
        functools.partial(right_kernel, net, units, side, places),
        "right_product",
        shaped((len(places) * units, rank, LANES), dtype),
        [SMEM, SMEM, VMEM, VMEM, VMEM],
        4,
        0.7 * len(places),
        out_specs=VMEM,
    )(*place, in_vmem(comp), near, far)


def new_error_kernel(net, units, blocks, rows_too, dp, mp, comp, near, far, *rest):
    place = Place(net, (dp, mp))
    rights, rest = rest[: len(blocks)], rest[len(blocks) :]
    count = comp.shape[0] // 2
    copies = []
    if rows_too:
        own, other, _, out, factor_rows, buf, sems, rows_buf, rows_sem = rest
        for side, source in ((NEAR, own), (FAR, other)):
            start = place.half(side) * (units * LANES)
            for i in range(units):
                rows_buf[pl.ds(pl.multiple_of(start + i * LANES, LANES), LANES), :] = source[i].T
        copies.append(pltpu.make_async_copy(rows_buf, factor_rows, rows_sem))
        copies[0].start()
    else:
        out, buf, sems = rest[-3:]
    step = min(128, count)
    for j, ((side, k), right) in enumerate(zip(blocks, rights)):
        start = place.block(side, k) * (units * LANES)
        for half, base in enumerate((near, far)):
            rows = pl.ds(pl.multiple_of(place.half(half) * count, count), count)
            for unit in range(0, units, 2):
                wide = min(2, units - unit)
                factor = [right[unit + i] for i in range(wide)]
                factor = jnp.concatenate(factor, axis=1) if wide > 1 else factor[0]
                at = pl.ds(pl.multiple_of(start + unit * LANES, LANES), wide * LANES)
                here = pl.ds(unit * LANES, wide * LANES)
                for row in range(0, count, step):
                    product = jnp.dot(base[row : row + step], factor, preferred_element_type=F32)
                    kept = comp[half * count + row : half * count + row + step, at].astype(F32)
                    buf[half, j, row : row + step, here] = (kept - product).astype(BF16)
                copy = pltpu.make_async_copy(
                    buf.at[half, j, :, here], out.at[rows, at], sems.at[half, j, unit // 2]
                )
                copy.start()
                copies.append(copy)
    for copy in copies:
        copy.wait()


def new_error(net, place, blocks, rights, units, comp, near, far, held=None, block_0=()):
    rows, cols = comp.shape
    rank = near.shape[1]
    outs, scratch = [shaped((rows, cols), BF16)], [
        pltpu.VMEM((2, len(blocks), rows // 2, units * LANES), BF16),
        pltpu.SemaphoreType.DMA((2, len(blocks), (units + 1) // 2)),
    ]
    if block_0:
        outs.append(shaped((2 * units * LANES, rank), BF16))
        scratch += [pltpu.VMEM((2 * units * LANES, rank), BF16), pltpu.SemaphoreType.DMA]
    held = [] if held is None else [in_hbm(held)]
    out = call(
        functools.partial(new_error_kernel, net, units, blocks, len(block_0)),
        "new_error",
        outs,
        [SMEM] * 2 + [VMEM] * (3 + len(blocks) + len(block_0)) + [HBM] * len(held),
        12,
        0.6 + 0.8 * len(blocks),
        out_specs=[HBM] * len(outs),
        scratch_shapes=scratch,
        input_output_aliases={5 + len(blocks) + len(block_0): 0} if held else {},
    )(*place, in_vmem(comp), near, far, *rights, *block_0, *held)
    return out if block_0 else out[0]


def leaf_steps(state, leaf):
    n, b = state.shape[0], LEAF
    base = leaf * b

    def splat(v):
        return jnp.broadcast_to(v, (b, n))

    def column(tile, j):
        return splat(state[b * tile : b * tile + b, base + j : base + j + 1])

    here = [column(leaf, j) for j in range(b)]
    a = [[splat(here[j][i : i + 1]) if j <= i else None for j in range(b)] for i in range(b)]
    mult = [[None] * b for _ in range(b)]
    unit = [[None] * b for _ in range(b)]
    recip, scale = [], []
    for k in range(b):
        recip.append(1.0 / a[k][k])
        scale.append(lax.rsqrt(a[k][k]))
        for i in range(k + 1, b):
            mult[i][k] = a[i][k] * recip[k]
        for i in range(k + 1, b):
            for j in range(k + 1, i + 1):
                a[i][j] = a[i][j] - mult[i][k] * a[j][k]
    for j in range(b):
        for i in range(j + 1, b):
            total = mult[i][j]
            for k in range(j + 1, i):
                total = total + mult[i][k] * unit[k][j]
            unit[i][j] = -total
    rows_x = [splat(state[base + j : base + j + 1, n:]) for j in range(b)]
    if leaf + 1 < n // b:
        rows_g = [splat(state[base + j : base + j + 1, :n]) for j in range(b)]

        def term(k, j):
            return recip[k] if j == k else recip[k] * unit[k][j]

        inverse = [[None] * b for _ in range(b)]
        for i in range(b):
            for j in range(i + 1):
                total = term(i, j)
                for k in range(i + 1, b):
                    total = total + unit[k][i] * term(k, j)
                inverse[i][j] = inverse[j][i] = total

        def mixed(rows):
            out = []
            for k in range(b):
                total = inverse[k][0] * rows[0]
                for j in range(1, b):
                    total = total + inverse[k][j] * rows[j]
                out.append(total)
            return out

        mixed_g, mixed_x = mixed(rows_g), mixed(rows_x)
        for tile in range(leaf + 1, n // b):
            at = slice(b * tile, b * tile + b)
            columns = [column(tile, j) for j in range(b)]
            g, x = state[at, :n], state[at, n:]
            for k in range(b):
                g = g - columns[k] * mixed_g[k]
                x = x - columns[k] * mixed_x[k]
            state[at, :n] = g
            state[at, n:] = x
    for i in range(b):
        total = rows_x[i]
        for j in range(i):
            total = total + unit[i][j] * rows_x[j]
        state[base + i : base + i + 1, n:] = (total * scale[i])[:1]


def inverse_kernel(gram, state):
    n = state.shape[0]
    state[:, :n] = gram[...]
    row = lax.broadcasted_iota(jnp.int32, (n, n), 0)
    state[:, n:] = (row == lax.broadcasted_iota(jnp.int32, (n, n), 1)).astype(F32)
    for leaf in range(n // LEAF):
        leaf_steps(state, leaf)


def inverse_of(gram):
    n = gram.shape[0]
    return call(inverse_kernel, "inverse", shaped((n, 2 * n), F32), [VMEM], 4, 4.5, out_specs=VMEM)(gram)


def split2(x):
    high = x.astype(BF16)
    return high, (x - high.astype(F32)).astype(BF16)


def first_kernel(part, across, near, far, out, gram):
    units = part.shape[0]
    contract = (((1,), (1,)), ((), ()))
    total = lax.dot_general(near[...], near[...], contract, preferred_element_type=F32)
    total += lax.dot_general(far[...], far[...], contract, preferred_element_type=F32)
    out[units], out[units + 1] = split2(total)
    gram[...] = out[units].astype(F32) + out[units + 1].astype(F32)
    for i in range(units):
        out[i] = (part[i] + across[i].astype(F32)).astype(BF16)


def second_kernel(part, across, arrived, out):
    for i in range(out.shape[0]):
        out[i] = (part[i] + across[i].astype(F32) + arrived[i].astype(F32)).astype(BF16)


def kept_kernel(part, across, arrived, gram_in, out, gram):
    units = out.shape[0]
    gram[...] = gram_in[...] + (arrived[units].astype(F32) + arrived[units + 1].astype(F32))
    for i in range(units):
        out[i] = part[i] + across[i].astype(F32) + arrived[i].astype(F32)


def add_kernel(one, other, out):
    for i in range(one.shape[0]):
        out[i] = (one[i].astype(F32) + other[i].astype(F32)).astype(BF16)


def factor_kernel(replicas, own, arrived, state, out):
    units, rank = own.shape[:2]
    lhs = jnp.concatenate(split2(state[:, rank:]), axis=0)
    for i in range(0, units, 2):
        some = range(i, min(i + 2, units))
        summed = [(own[k].astype(F32) + arrived[k].astype(F32)).astype(BF16) for k in some]
        summed = jnp.concatenate(summed, axis=1) if len(summed) > 1 else summed[0]
        product = jnp.dot(lhs, summed, preferred_element_type=F32)
        product = (product[:rank] + product[rank:]) / replicas
        for k in some:
            out[k] = product[:, (k - i) * LANES : (k - i + 1) * LANES].astype(BF16)


def base_kernel(near, far, state, near_out, far_out):
    rank = near.shape[0]
    lhs = jnp.concatenate(split2(state[:, rank:]), axis=0)
    for source, out in ((near, near_out), (far, far_out)):
        product = jnp.dot(lhs, source[...], preferred_element_type=F32)
        out[...] = (product[:rank] + product[rank:]).T.astype(BF16)


class Exchange:
    def __init__(self, dp, mp):
        self.dp, self.mp = dp, mp
        mp_bits = [("mp", 1 << k) for k in range(mp.bit_length() - 1)]
        z_bits = [("dp", 2 << k) for k in range(dp.bit_length() - 2)]
        low, high = mp_bits[0], mp_bits[len(mp_bits) // 2]
        self.other = [bit for bit in mp_bits if bit not in (low, high)]
        self.scatter = [(low, high), (high, low)]
        rest = self.other + z_bits
        self.rest = list(zip(rest[::-1], rest))
        self.replicas = list(zip(z_bits, z_bits[::-1]))
        self.low, self.high = low, high

    def send(self, x, step):
        pairs = []
        for d in range(self.dp):
            for m in range(self.mp):
                axis, bit = step[d % 2]
                to = (d ^ bit) * self.mp + m if axis == "dp" else d * self.mp + (m ^ bit)
                pairs.append((d * self.mp + m, to))
        return lax.ppermute(x, AXES, pairs)

    def core(self, x):
        return self.send(x, (("dp", 1), ("dp", 1)))


def on_device(dp, mp, grad, error, init):
    grad, error = grad[0], error[0]
    rows, cols = grad.shape
    rank = init.shape[1]
    net = Exchange(dp, mp)
    place = [lax.axis_index(axis).astype(jnp.int32).reshape(1) for axis in AXES]
    units = cols // 8 // LANES
    square = (rank, LANES)

    comp, near, far = left_product(net, place, grad, error, init)
    near = near + net.core(far)
    for step in net.replicas:
        sent = lax.reduce_precision(near, 8, 7)
        near = sent + net.send(sent.astype(BF16), step).astype(F32)
    near = near.astype(BF16)
    far = net.core(near)

    def right(side, places, dtype):
        return right_product(net, place, side, places, units, comp, near, far, dtype)

    def small(kernel, name, outs, *ins):
        return call(kernel, name, outs, [VMEM] * len(ins), 4, 0.3, out_specs=jax.tree.map(lambda _: VMEM, outs))(*ins)

    block, square_f32 = shaped((units, *square), BF16), shaped((rank, rank), F32)
    across_3 = net.core(right(FAR, (3,), BF16))
    across_2 = net.core(right(FAR, (2,), BF16))
    sent = small(add_kernel, "first_sum", block, right(NEAR, (3,), F32), across_3)
    near, far, sent = lax.optimization_barrier((near, far, sent))
    arrived_1 = net.send(sent, net.scatter[0])
    sent, gram = small(
        first_kernel, "first_sum", [shaped((units + 2, *square), BF16), square_f32],
        right(NEAR, (2,), F32), across_2, near, far,
    )
    near, far, sent = lax.optimization_barrier((near, far, sent))
    arrived_0 = net.send(sent, net.scatter[0])
    across = net.core(right(FAR, (1,), BF16))
    part = right(NEAR, (1,), F32)
    near, far, arrived_1 = lax.optimization_barrier((near, far, arrived_1))
    sent = small(second_kernel, "second_sum", block, part, across, arrived_1)
    across = net.core(right(FAR, (0,), BF16))
    part = right(NEAR, (0,), F32)
    arrived = net.send(sent, net.scatter[1])
    kept, gram = small(
        kept_kernel, "second_sum", [shaped((units, *square), F32), square_f32], part, across, arrived_0, gram
    )
    gram = gram + net.send(gram, net.scatter[1])
    for bit in net.other:
        gram = gram + net.send(gram, (bit, bit))
    sent = small(add_kernel, "third_sum", block, kept, arrived)

    for step in net.rest[:-1]:
        arrived, gram = lax.optimization_barrier((net.send(sent, step), gram))
        sent = small(add_kernel, "pair_sum", block, sent, arrived)
    arrived = net.send(sent, net.rest[-1])
    sent, gram = lax.optimization_barrier((sent, gram))
    state = inverse_of(gram)
    base_near, base_far = small(base_kernel, "base", [shaped((rows // 2, rank), BF16)] * 2, near, far, state)
    arrived, state, base_near, base_far = lax.optimization_barrier((arrived, state, base_near, base_far))
    own = small(functools.partial(factor_kernel, dp), "factor", block, sent, arrived, state)

    blocks = [own, net.send(own, net.scatter[1]), net.send(own, net.scatter[0]), None]
    write = functools.partial(new_error, net, place, units=units, comp=comp, near=base_near, far=base_far)
    out = write([(NEAR, 0)], [own])
    own, out = lax.optimization_barrier((own, out))
    others = [net.core(own)]
    blocks[1], out = lax.optimization_barrier((blocks[1], out))
    blocks[3] = net.send(blocks[1], net.scatter[0])
    others.append(net.core(blocks[1]))
    blocks[2], out = lax.optimization_barrier((blocks[2], out))
    others.append(net.core(blocks[2]))
    share, width = cols // mp, units * LANES
    right_factor = None
    some = [(FAR, 0), (NEAR, 1), (FAR, 1), (NEAR, 2)], [others[0], blocks[1], others[1], blocks[2]]
    if share == 2 * width:
        out, right_factor = write(*some, held=out, block_0=(own, others[0]))
    else:
        out = write(*some, held=out)
    blocks[3], out = lax.optimization_barrier((blocks[3], out))
    others.append(net.core(blocks[3]))
    out = write([(FAR, 2), (NEAR, 3)], [others[2], blocks[3]], held=out)
    out = write([(FAR, 3)], [others[3]], held=out)
    if right_factor is None:
        everything = jnp.concatenate(blocks + others, axis=0)
        here = Place(net, place)
        names = jnp.stack([here.block(side, k) for side in (NEAR, FAR) for k in range(4)])
        block = here.mp * share // width
        chosen = lax.dynamic_slice_in_dim(everything, jnp.argmax(names == block) * units, units, 0)
        chosen = jnp.swapaxes(chosen, 1, 2).reshape(width, rank)
        right_factor = lax.dynamic_slice_in_dim(chosen, here.mp * share - block * width, share, 0)
    return (out[None], right_factor)


def solution(mesh):
    return jax.shard_map(
        functools.partial(on_device, mesh.shape["dp"], mesh.shape["mp"]),
        mesh=mesh,
        in_specs=(P("dp", "mp", None), P("dp", "mp", None), P()),
        out_specs=(P("dp", "mp", None), P("mp", None)),
        check_vma=False,
    )
```
